128 devices in a mesh: group: 16 (over y, z_hi, core), dom: 8 (over x, z_lo).
Axes of the slice: x: 4, y: 4, z: 4 (z_hi: 2, z_lo: 2; z = z_hi * 2 + z_lo), core: 2. Of those that a mesh axis runs over, the one named last changes fastest.
Arguments:
- head: float32 [16, 128, 128, 512], P('group', 'dom'), may hold values from -4 to 4
- conductivity: float32 [16, 128, 128, 512], P('group', 'dom'), may hold values from 0.2 to 2
- coarse_conductivity: float32 [16, 64, 64, 256], P('group', 'dom'), may hold values from 0.2 to 2
- pairing: int32 [16], replicated, may hold values from 0 to 15, as said below
Outputs:
- fine_next: float32 [16, 128, 128, 512], P('group', 'dom')
- coarse_next: float32 [16, 64, 64, 256], P('group', 'dom')
- difference: float32 [16, 64, 64, 256], P('group', 'dom')
The draws below stay inside these ranges and needn't reach their ends.
Inputs may be any that keep to these rules, and one draw needn't show every extreme that they name: `pairing`: each sample index appears exactly once.
All inputs are finite; a program needn't handle non-finite values.
Results may differ from the reference program's by a relative error of at most 0.0003.
Values sent between devices are 32-bit elements; how exact they have to be, the bound alone decides.
A program may use at most 128 MiB of HBM per device.

```python
import math
import jax
import jax.numpy as jnp
from jax import lax

NY = 128
NZ = 512
G = 16
NX = 128


def place_value(perm, position, target):
    current = perm[position]
    swapped = jnp.where(perm == target, current, perm)
    return swapped.at[position].set(target)


def draw_pairing(key, part):
    key = jax.random.fold_in(key, 7)
    perm_key, start_key = jax.random.split(key)
    perm = jax.random.permutation(perm_key, G).astype(jnp.int32)
    first = jax.random.randint(start_key, (), 0, G).astype(jnp.int32)
    second = (first + 1) % G
    third = (first + 2) % G
    perm = place_value(perm, first, (first + G - 1) % G)
    perm = place_value(perm, second, (second + 1) % G)
    perm = place_value(perm, third, (third + G // 2) % G)
    return perm.astype(jnp.int32)


def level_of(own_key, shape, pieces, smallest, largest):
    def one(dim, parts):
        draws = jax.random.uniform(jax.random.fold_in(jax.random.fold_in(own_key, 6), dim), (parts,), jnp.float32, smallest / len(pieces), largest / len(pieces))
        return jnp.repeat(jnp.exp(draws), shape[dim] // parts).reshape((-1,) + (1,) * (len(shape) - dim - 1))

    factor_of = one(*pieces[0])
    for cut in pieces[1:]:
        factor_of = factor_of * one(*cut)
    return factor_of


def gaussian(stream_key, shape, scale, reach, cuts=(), kind=jnp.bfloat16):
    values = scale * jax.random.normal(stream_key, shape, jnp.float32)
    if cuts:
        values = values * level_of(stream_key, shape, cuts, -0.22, 0.18)
    return jnp.clip(values, -reach, reach).astype(kind)


def setup_inputs(seed: int = 0) -> dict:
    keys = jax.random.split(jax.random.key(seed), 5)
    return {
        "head": gaussian(keys[0], (G, NX, NY, NZ), 1.0, 4.0, ((0, 16), (1, 8)), jnp.float32),
        "conductivity": jnp.clip(jnp.exp(math.log(2.0) - 2.3025851 * jax.random.uniform(keys[1], (G, NX, NY, NZ), jnp.float32) ** level_of(keys[1], (G, NX, NY, NZ), ((0, 16), (1, 8)), -0.2, 0.2)), 0.2, 2.0),
        "coarse_conductivity": jnp.clip(jnp.exp(math.log(2.0) - 2.3025851 * jax.random.uniform(keys[2], (G, NX // 2, NY // 2, NZ // 2), jnp.float32) ** level_of(keys[2], (G, NX // 2, NY // 2, NZ // 2), ((0, 16), (1, 8)), -0.2, 0.2)), 0.2, 2.0),
        "pairing": draw_pairing(jax.random.fold_in(keys[4], 71), 0),
    }


alpha_vg = 1.5
theta_span = 0.4
storage = 0.5
step_dt = 0.05

def closure(head, cond):
    neg = jnp.minimum(head, 0.0)
    usq = alpha_vg * neg * (alpha_vg * neg)
    wet = 1.0 / jnp.sqrt(1.0 + usq)
    rel = jnp.sqrt(wet) * (1.0 - jnp.sqrt(usq / (1.0 + usq))) ** 2
    cap = storage + theta_span * alpha_vg * alpha_vg * -neg * wet * wet * wet
    return (cond * rel, cap)

def advance(padded_h, padded_k, head, keff, cap, spacing):
    total = jnp.zeros_like(head)
    shifts = [((2, None), (1, -1), (1, -1), 0.0), ((0, -2), (1, -1), (1, -1), 0.0), ((1, -1), (2, None), (1, -1), 0.0), ((1, -1), (0, -2), (1, -1), 0.0), ((1, -1), (1, -1), (2, None), spacing), ((1, -1), (1, -1), (0, -2), -spacing)]
    for first, second, third, lift in shifts:
        near_h = padded_h[first[0]:first[1], second[0]:second[1], third[0]:third[1]]
        near_k = padded_k[first[0]:first[1], second[0]:second[1], third[0]:third[1]]
        total = total + 0.5 * (near_k + keff) * (near_h - head + lift)
    return head + step_dt * total / (spacing * spacing * cap)

def restrict(field):
    a, b, c = field.shape
    return lax.optimization_barrier(jnp.mean(field.reshape(a // 2, 2, b // 2, 2, c // 2, 2), axis=(1, 3, 5)))

def one_step(head, cond, spacing):
    keff, cap = closure(head, cond)
    return advance(jnp.pad(head, 1), jnp.pad(keff, 1), head, keff, cap, spacing)

def reference(head, conductivity, coarse_conductivity, pairing):

    def fine_work(pair_in):
        new = one_step(pair_in[0], pair_in[1], 1.0)
        return (new, restrict(pair_in[0]), restrict(new))
    fine_next, start_small, next_small = lax.map(fine_work, (head, conductivity))
    coarse_start = start_small[pairing]
    coarse_next = lax.map(lambda pair_in: one_step(pair_in[0], pair_in[1], 2.0), (coarse_start, coarse_conductivity))
    difference = next_small[pairing] - coarse_next
    return (fine_next, coarse_next, difference)
```

```python
import functools

import jax
import jax.numpy as jnp
from jax import lax
from jax.experimental import pallas as pl
from jax.experimental.pallas import tpu as pltpu
from jax.sharding import PartitionSpec as P

MESH = pl.DeviceIdType.MESH
F32 = jnp.float32
NP = 8
CAP = 8

TOP = 8
CH = 32


def place(layer):
    return {0: 0, 7: 1}.get(layer, layer + 1)


def closure(h, cond, spacing):
    t = 1.5 * jnp.minimum(h, 0.0)
    r = lax.rsqrt(1.0 + t * t)
    p = t * r
    a = 1.0 + p
    k = cond * (r * lax.rsqrt(r) * (a * a))
    s2 = spacing * spacing
    w = 1.0 / (20.0 * s2 - (24.0 * s2) * (p * (r * r)))
    return k, w


def in_layer(hb, kb, x, row, rows, spacing):
    ha = hb[x, pl.ds(row, rows + 16), :]
    ka = kb[x, pl.ds(row, rows + 16), :]
    h, k = ha[8 : 8 + rows], ka[8 : 8 + rows]
    tot = (ka[9 : 9 + rows] + k) * (ha[9 : 9 + rows] - h)
    hd, kd = ha[7 : 7 + rows], ka[7 : 7 + rows]
    tot = tot + (kd + k) * (hd - h)
    n = h.shape[1]
    lane = lax.broadcasted_iota(jnp.int32, h.shape, 1)
    hz = jnp.where(lane == n - 1, 0.0, pltpu.roll(h, n - 1, 1))
    kz = jnp.where(lane == n - 1, 0.0, pltpu.roll(k, n - 1, 1))
    hs = h - spacing
    fz = (kz + k) * (hz - hs)
    fd = jnp.where(lane == 0, k * (h + spacing), pltpu.roll(fz, 1, 1))
    return h, k, tot + (fz - fd)


def kernel(cap, pairing, head, cond, ccond, fine_out, coarse_out, diff_out,
           hb, kb, wb, fx, f01, frecv, vs, pick,
           sbuf, sab, sx, sy, sc, sd, nbuf, nab, nx, ny, nc, nd, bbuf, bab, bx, by, bc, bd,
           ch, ck, cw, cfx, cf01, cfrecv, dbuf,
           hsem, ksem, csem, osem, halo_s, halo_r, sa_s, sa_r, na_s, na_r, ba_s, ba_r, sc_s, sc_r, nc_s, nc_r, bc_s, bc_r,
           cross_s, cross_r):
    g = lax.axis_index("group")
    d = lax.axis_index("dom")
    zh = lax.rem(g // 2, 2)
    me = (g // 4) * 2 + lax.rem(g, 2)

    def index_of(j, plane):
        return (j // 2) * 4 + plane * 2 + lax.rem(j, 2)

    def mate(s):
        j = lax.rem(me + s, NP)
        return j, index_of(j, zh)

    other = index_of(me, 1 - zh)
    last = 7

    def load(src, dst, sem):
        return pltpu.make_async_copy(src, dst, sem)

    def hload(l):
        return load(head.at[0, pl.ds(2 * l, 2)], hb.at[pl.ds(2 * l, 2), pl.ds(TOP, 128), :], hsem.at[l])

    def kload(l):
        return load(cond.at[0, pl.ds(2 * l, 2)], kb.at[pl.ds(2 * l, 2), pl.ds(TOP, 128), :], ksem.at[l])

    cload = load(ccond.at[0], ck.at[pl.ds(0, 8), pl.ds(8, 64), :], csem)
    hload(0).start()
    kload(0).start()
    for l in range(1, 8):
        hload(l).start()
    for l in range(1, 8):
        kload(l).start()
    cload.start()

    bar = pltpu.get_barrier_semaphore()

    def greet(g2, d2):
        pl.semaphore_signal(bar, inc=1, device_id=(g2, d2), device_id_type=MESH)

    for s in range(1, NP):
        greet(mate(s)[1], d)
    greet(other, d)

    @pl.when(d > 0)
    def _():
        greet(g, d - 1)

    @pl.when(d < last)
    def _():
        greet(g, d + 1)

    z8 = jnp.zeros((8, 512), F32)
    zc = jnp.zeros((8, 256), F32)

    def pads(x, _):
        for b in (hb, kb):
            b[x, 0:8, :] = z8
            b[x, 136:144, :] = z8
        return 0

    lax.fori_loop(0, 16, pads, 0)

    def cpads(x, _):
        for b in (ch, ck):
            b[x, 0:8, :] = zc
            b[x, 72:80, :] = zc
        return 0

    lax.fori_loop(0, 8, cpads, 0)
    pi = lax.broadcasted_iota(jnp.int32, (256, 128), 0)
    pj = lax.broadcasted_iota(jnp.int32, (256, 128), 1)
    pick[...] = jnp.where(pi // 2 == pj, 0.125, 0.0).astype(jnp.bfloat16)

    @pl.when(d == last)
    def _():
        def zero(i, _):
            hb[16, pl.ds(TOP + i * 8, 8), :] = z8
            kb[16, pl.ds(TOP + i * 8, 8), :] = z8
            return 0

        lax.fori_loop(0, 16, zero, 0)

        def czero(i, _):
            ch[8, pl.ds(8 + i * 8, 8), :] = zc
            ck[8, pl.ds(8 + i * 8, 8), :] = zc
            return 0

        lax.fori_loop(0, 8, czero, 0)

    cross = [jnp.int32(0)] * cap
    count = jnp.int32(0)
    for j in range(NP):
        p = pairing[index_of(j, 1 - zh)]
        mine = lax.rem(p // 2, 2) == zh
        slot = (p // 4) * 2 + lax.rem(p, 2)
        for i in range(cap):
            cross[i] = jnp.where(mine & (count == i), slot, cross[i])
        count = count + jnp.where(mine, 1, 0)
    where = []
    count = jnp.int32(0)
    for j in range(NP):
        p = pairing[index_of(j, zh)]
        mine = lax.rem(p // 2, 2) == zh
        where.append((mine, (p // 4) * 2 + lax.rem(p, 2), jnp.minimum(count, cap - 1)))
        count = count + jnp.where(mine, 0, 1)

    def close_layer(x):
        def body(i, _):
            r = pl.multiple_of(i * CH, CH)
            k, w = closure(hb[x, pl.ds(TOP + r, CH), :], kb[x, pl.ds(TOP + r, CH), :], 1.0)
            kb[x, pl.ds(TOP + r, CH), :] = k
            wb[x, pl.ds(r, CH), :] = w
            return 0

        lax.fori_loop(0, 128 // CH, body, 0)

    hload(0).wait()
    kload(0).wait()
    close_layer(0)
    pl.semaphore_wait(bar, NP + jnp.where(d > 0, 1, 0) + jnp.where(d < last, 1, 0))

    def remote(src, dst, ssem, rsem, g2, d2):
        return pltpu.make_async_remote_copy(src_ref=src, dst_ref=dst, send_sem=ssem, recv_sem=rsem,
                                            device_id=(g2, d2), device_id_type=MESH)

    down = d - 1
    upper = d + 1
    rows = pl.ds(TOP, 128)
    halo_h = remote(hb.at[0, rows, :], hb.at[16, rows, :], halo_s.at[0], halo_r.at[0], g, down)
    halo_k = remote(kb.at[0, rows, :], kb.at[16, rows, :], halo_s.at[1], halo_r.at[1], g, down)
    halo_f = remote(fx, frecv, halo_s.at[2], halo_r.at[2], g, upper)
    crow = pl.ds(8, 64)
    chalo_h = remote(ch.at[0, crow, :], ch.at[8, crow, :], halo_s.at[3], halo_r.at[3], g, down)
    chalo_k = remote(ck.at[0, crow, :], ck.at[8, crow, :], halo_s.at[4], halo_r.at[4], g, down)
    chalo_f = remote(cfx, cfrecv, halo_s.at[5], halo_r.at[5], g, upper)

    @pl.when(d > 0)
    def _():
        halo_h.start()
        halo_k.start()

    def restrict(a, b, store):
        for r in range(0, 128, CH):
            s = a(r) + b(r)
            for q in range(4):
                vs[q, r : r + CH, :] = s[:, q * 128 : (q + 1) * 128]
        for half in range(2):
            parts = [vs[q, pl.ds(0, 64, 2), :] + vs[q, pl.ds(1, 64, 2), :] for q in (2 * half, 2 * half + 1)]
            e = jnp.concatenate(parts, axis=1)
            hi = e.astype(jnp.bfloat16)
            lo = (e - hi.astype(F32)).astype(jnp.bfloat16)
            w = pick[...]
            o = jnp.dot(hi, w, preferred_element_type=F32) + jnp.dot(lo, w, preferred_element_type=F32)
            store(half, o)

    def into(buf, pos):
        def store(half, o):
            buf[:, pos, :, half * 128 : (half + 1) * 128] = o.reshape(8, 8, 128)

        return store

    def a_copy(s, buf, ab, ssem, rsem):
        j, g2 = mate(s)
        return remote(buf.at[j], ab.at[me], ssem.at[s - 1], rsem.at[s - 1], g2, d)

    def a_start(buf, ab, ssem, rsem):
        for s in range(1, NP):
            a_copy(s, buf, ab, ssem, rsem).start()
        ab[me] = buf[me]

    def a_wait(buf, ab, ssem, rsem):
        for s in range(1, NP):
            a_copy(s, buf, ab, ssem, rsem).wait()

    def b_copy(i, x, y):
        return remote(x, y, cross_s.at[i], cross_r.at[i], other, d)

    def b_start(i, x, y, ab):
        for n in range(cap):
            x[n] = ab[cross[n]]
        b_copy(i, x, y).start()

    def c_copy(s, buf, to, ssem, rsem):
        j, g2 = mate(s)
        return remote(buf.at[j], to.at[me], ssem.at[s - 1], rsem.at[s - 1], g2, d)

    def c_start(ab, y, buf, to, ssem, rsem):
        for j in range(NP):
            mine, slot, crossed = where[j]
            buf[j] = jnp.where(mine, ab[slot], y[crossed])
        for s in range(1, NP):
            c_copy(s, buf, to, ssem, rsem).start()
        to[me] = buf[me]

    def c_wait(buf, to, ssem, rsem):
        for s in range(1, NP):
            c_copy(s, buf, to, ssem, rsem).wait()

    for l in range(8):
        if l:
            hload(l).wait()
        restrict(lambda r: hb[2 * l, pl.ds(TOP + r, CH), :], lambda r: hb[2 * l + 1, pl.ds(TOP + r, CH), :], into(sbuf, place(l)))
    a_start(sbuf, sab, sa_s, sa_r)

    def face(x, r):
        here, there = (x, pl.ds(TOP + r, CH), slice(None)), (x + 1, pl.ds(TOP + r, CH), slice(None))
        return (kb[there] + kb[here]) * (hb[there] - hb[here])

    def step_layer(x):
        def body(i, _):
            r = pl.multiple_of(i * CH, CH)
            h, k, tot = in_layer(hb, kb, x, r, CH, 1.0)
            f = (kb[x + 1, pl.ds(TOP + r, CH), :] + k) * (hb[x + 1, pl.ds(TOP + r, CH), :] - h)
            tot = tot + (f - fx[pl.ds(r, CH), :])
            fx[pl.ds(r, CH), :] = f
            wb[x, pl.ds(r, CH), :] = h + tot * wb[x, pl.ds(r, CH), :]
            return 0

        lax.fori_loop(0, 128 // CH, body, 0)

    def out_pair(l):
        return load(wb.at[pl.ds(2 * l, 2)], fine_out.at[0, pl.ds(2 * l, 2)], osem.at[l])

    def out_row(x):
        return lambda r: wb[x, pl.ds(r, CH), :]

    def next_small(l, buf, pos):
        restrict(out_row(2 * l), out_row(2 * l + 1), into(buf, pos))
        out_pair(l).start()

    close_layer(1)

    def first_face(i, _):
        r = pl.multiple_of(i * CH, CH)
        f = face(0, r)
        f01[pl.ds(r, CH), :] = f
        fx[pl.ds(r, CH), :] = f
        return 0

    lax.fori_loop(0, 128 // CH, first_face, 0)
    kload(1).wait()
    close_layer(2)
    step_layer(1)
    for l in range(1, 7):
        close_layer(2 * l + 1)
        step_layer(2 * l)
        kload(l + 1).wait()
        close_layer(2 * l + 2)
        step_layer(2 * l + 1)
        next_small(l, nbuf, l - 1)
        if l == 3:
            a_wait(sbuf, sab, sa_s, sa_r)
            b_start(0, sx, sy, sab)
    a_start(nbuf, nab, na_s, na_r)
    b_copy(0, sx, sy).wait()
    c_start(sab, sy, sc, sd, sc_s, sc_r)
    close_layer(15)
    step_layer(14)

    @pl.when(d < last)
    def _():
        halo_h.wait_recv()
        halo_k.wait_recv()

    step_layer(15)

    @pl.when(d < last)
    def _():
        halo_f.start()

    next_small(7, bbuf, 1)
    a_wait(nbuf, nab, na_s, na_r)
    b_start(1, nx, ny, nab)

    c_wait(sc, sd, sc_s, sc_r)
    cload.wait()

    def close_coarse(l):
        h = sd[:, place(l)].reshape(64, 256)
        k, w = closure(h, ck[l, crow, :], 2.0)
        ch[l, crow, :] = h
        ck[l, crow, :] = k
        cw[l] = w

    close_coarse(0)

    @pl.when(d > 0)
    def _():
        chalo_h.start()
        chalo_k.start()

    for l in range(1, 8):
        close_coarse(l)

    @pl.when(d > 0)
    def _():
        halo_f.wait_recv()

    @pl.when(d == 0)
    def _():
        def edge(i, _):
            r = pl.multiple_of(i * CH, CH)
            frecv[pl.ds(r, CH), :] = hb[0, pl.ds(TOP + r, CH), :] * kb[0, pl.ds(TOP + r, CH), :]
            return 0

        lax.fori_loop(0, 128 // CH, edge, 0)

    def lowest(i, _):
        r = pl.multiple_of(i * CH, CH)
        h, k, tot = in_layer(hb, kb, 0, r, CH, 1.0)
        tot = tot + (f01[pl.ds(r, CH), :] - frecv[pl.ds(r, CH), :])
        wb[0, pl.ds(r, CH), :] = h + tot * wb[0, pl.ds(r, CH), :]
        return 0

    lax.fori_loop(0, 128 // CH, lowest, 0)
    next_small(0, bbuf, 0)
    a_start(bbuf, bab, ba_s, ba_r)

    b_copy(1, nx, ny).wait()
    c_start(nab, ny, nc, nd, nc_s, nc_r)

    def cface(x):
        return (ck[x + 1, crow, :] + ck[x, crow, :]) * (ch[x + 1, crow, :] - ch[x, crow, :])

    def step_coarse(x):
        h, k, tot = in_layer(ch, ck, x, 0, 64, 2.0)
        f = cface(x)
        tot = tot + (f - cfx[...])
        cfx[...] = f
        cw[x] = h + tot * cw[x]

    f = cface(0)
    cf01[...] = f
    cfx[...] = f
    for x in range(1, 7):
        step_coarse(x)

    @pl.when(d < last)
    def _():
        chalo_h.wait_recv()
        chalo_k.wait_recv()

    step_coarse(7)

    @pl.when(d < last)
    def _():
        chalo_f.start()

    a_wait(bbuf, bab, ba_s, ba_r)
    b_start(2, bx, by, bab)

    @pl.when(d > 0)
    def _():
        chalo_f.wait_recv()

    @pl.when(d == 0)
    def _():
        cfrecv[...] = ch[0, crow, :] * ck[0, crow, :]

    h, k, tot = in_layer(ch, ck, 0, 0, 64, 2.0)
    tot = tot + (cf01[...] - cfrecv[...])
    cw[0] = h + tot * cw[0]
    cout = load(cw, coarse_out.at[0], csem)
    cout.start()
    b_copy(2, bx, by).wait()
    c_start(bab, by, bc, bd, bc_s, bc_r)
    c_wait(nc, nd, nc_s, nc_r)
    for l in range(1, 7):
        dbuf[l] = nd[:, l - 1].reshape(64, 256) - cw[l]
    c_wait(bc, bd, bc_s, bc_r)
    dbuf[0] = bd[:, 0].reshape(64, 256) - cw[0]
    dbuf[7] = bd[:, 1].reshape(64, 256) - cw[7]
    dout = load(dbuf, diff_out.at[0], ksem.at[0])
    dout.start()

    @pl.when(d > 0)
    def _():
        halo_h.wait_send()
        halo_k.wait_send()
        chalo_h.wait_send()
        chalo_k.wait_send()

    @pl.when(d < last)
    def _():
        halo_f.wait_send()
        chalo_f.wait_send()

    for l in range(8):
        out_pair(l).wait()
    cout.wait()
    dout.wait()


def payload(cap, layers):
    piece = (layers, 8, 256)
    return [
        pltpu.VMEM((NP,) + piece, F32),
        pltpu.VMEM((NP,) + piece, F32),
        pltpu.VMEM((cap,) + piece, F32),
        pltpu.VMEM((cap,) + piece, F32),
        pltpu.VMEM((NP,) + piece, F32),
        pltpu.VMEM((NP,) + piece, F32),
    ]


def run(cap, pairing, head, cond, ccond):
    dma = pltpu.SemaphoreType.DMA
    scratch = [
        pltpu.VMEM((17, 144, 512), F32),
        pltpu.VMEM((17, 144, 512), F32),
        pltpu.VMEM((16, 128, 512), F32),
        pltpu.VMEM((128, 512), F32),
        pltpu.VMEM((128, 512), F32),
        pltpu.VMEM((128, 512), F32),
        pltpu.VMEM((4, 128, 128), F32),
        pltpu.VMEM((256, 128), jnp.bfloat16),
        *payload(cap, 8),
        *payload(cap, 6),
        *payload(cap, 2),
        pltpu.VMEM((9, 80, 256), F32),
        pltpu.VMEM((9, 80, 256), F32),
        pltpu.VMEM((8, 64, 256), F32),
        pltpu.VMEM((64, 256), F32),
        pltpu.VMEM((64, 256), F32),
        pltpu.VMEM((64, 256), F32),
        pltpu.VMEM((8, 64, 256), F32),
        dma((8,)), dma((8,)), dma, dma((8,)), dma((6,)), dma((6,)),
        *[dma((NP - 1,))] * 12,
        dma((3,)), dma((3,)),
    ]
    anywhere = pl.BlockSpec(memory_space=pl.ANY)
    return pl.pallas_call(
        functools.partial(kernel, cap),
        out_shape=(
            jax.ShapeDtypeStruct(head.shape, F32),
            jax.ShapeDtypeStruct(ccond.shape, F32),
            jax.ShapeDtypeStruct(ccond.shape, F32),
        ),
        in_specs=[pl.BlockSpec(memory_space=pltpu.SMEM), anywhere, anywhere, anywhere],
        out_specs=(anywhere, anywhere, anywhere),
        scratch_shapes=scratch,
        compiler_params=pltpu.CompilerParams(
            collective_id=0, has_side_effects=True, vmem_limit_bytes=48 * 2**20
        ),
    )(pairing, head, cond, ccond)


def per_device(head, conductivity, coarse_conductivity, pairing):
    return run(CAP, pairing, head, conductivity, coarse_conductivity)


def solution(mesh):
    block = P("group", "dom", None, None)
    return jax.shard_map(
        per_device,
        mesh=mesh,
        in_specs=(block, block, block, P()),
        out_specs=(block, block, block),
        check_vma=False,
    )
```

```python
import functools

import jax
import jax.numpy as jnp
from jax import lax
from jax.experimental import pallas as pl
from jax.experimental.pallas import tpu as pltpu
from jax.sharding import PartitionSpec as P

MESH = pl.DeviceIdType.MESH
F32 = jnp.float32
NP = 8
CAPS = (4, 5, 6, 8)

TOP = 8
CH = 32
NH = 2


FIRST = (0, 7, 1, 2)
SECOND = (3, 4, 5, 6)


def closure(h, cond, spacing):
    t = 1.5 * jnp.minimum(h, 0.0)
    r = lax.rsqrt(1.0 + t * t)
    p = t * r
    a = 1.0 + p
    k = cond * (r * lax.rsqrt(r) * (a * a))
    s2 = spacing * spacing
    w = 1.0 / (20.0 * s2 - (24.0 * s2) * (p * (r * r)))
    return k, w


def in_layer(hb, kb, x, row, rows, spacing):
    ha = hb[x, pl.ds(row, rows + 16), :]
    ka = kb[x, pl.ds(row, rows + 16), :]
    h, k = ha[8 : 8 + rows], ka[8 : 8 + rows]
    tot = (ka[9 : 9 + rows] + k) * (ha[9 : 9 + rows] - h)
    hd, kd = ha[7 : 7 + rows], ka[7 : 7 + rows]
    tot = tot + (kd + k) * (hd - h)
    n = h.shape[1]
    lane = lax.broadcasted_iota(jnp.int32, h.shape, 1)
    hz = jnp.where(lane == n - 1, 0.0, pltpu.roll(h, n - 1, 1))
    kz = jnp.where(lane == n - 1, 0.0, pltpu.roll(k, n - 1, 1))
    hs = h - spacing
    fz = (kz + k) * (hz - hs)
    fd = jnp.where(lane == 0, k * (h + spacing), pltpu.roll(fz, 1, 1))
    return h, k, tot + (fz - fd)


def kernel(cap, pairing_in, head, cond, ccond, fine_out, coarse_out, diff_out,
           hb, kb, wb, fx, f01, f15, frecv, vs, pick, pairing,
           sbuf, sab, sx, sy, sc, sd, tbuf, tab, tx, ty, tc, td, nbuf, nab, nx, ny, nc, nd, mbuf, mab, mx, my, mc, md, bbuf, bab, bx, by, bc, bd,
           ch, ck, cw, cfx, cf01, cf7, cfrecv, dbuf,
           hsem, ksem, csem, osem, halo_s, halo_r, sa_s, sa_r, ta_s, ta_r, na_s, na_r, ma_s, ma_r, ba_s, ba_r, sc_s, sc_r, tc_s, tc_r, nc_s, nc_r, mc_s, mc_r, bc_s, bc_r,
           cross_s, cross_r, psem):
    g = lax.axis_index("group")
    d = lax.axis_index("dom")
    zh = lax.rem(g // 2, 2)
    me = (g // 4) * 2 + lax.rem(g, 2)

    def index_of(j, plane):
        return (j // 2) * 4 + plane * 2 + lax.rem(j, 2)

    def mate(s):
        j = lax.rem(me + s, NP)
        return j, index_of(j, zh)

    other = index_of(me, 1 - zh)
    last = 7

    def load(src, dst, sem):
        return pltpu.make_async_copy(src, dst, sem)

    def hload(l):
        return load(head.at[0, pl.ds(2 * l, 2)], hb.at[pl.ds(2 * l, 2), pl.ds(TOP, 128), :], hsem.at[l])

    def kload(l):
        return load(cond.at[0, pl.ds(2 * l, 2)], kb.at[pl.ds(2 * l, 2), pl.ds(TOP, 128), :], ksem.at[l])

    cload = load(ccond.at[0], ck.at[pl.ds(0, 8), pl.ds(8, 64), :], csem)
    pload = load(pairing_in, pairing, psem)
    hload(0).start()
    kload(0).start()
    pload.start()
    for l in range(1, 8):
        hload(l).start()
    for l in range(1, 8):
        kload(l).start()
    cload.start()

    bar = pltpu.get_barrier_semaphore()

    def greet(g2, d2):
        pl.semaphore_signal(bar, inc=1, device_id=(g2, d2), device_id_type=MESH)

    for s in range(1, NP):
        greet(mate(s)[1], d)
    greet(other, d)

    @pl.when(d > 0)
    def _():
        greet(g, d - 1)

    @pl.when(d < last)
    def _():
        greet(g, d + 1)

    z8 = jnp.zeros((8, 512), F32)
    zc = jnp.zeros((8, 256), F32)

    def pads(x, _):
        for b in (hb, kb):
            b[x, 0:8, :] = z8
            b[x, 136:144, :] = z8
        return 0

    lax.fori_loop(0, 16, pads, 0)

    def cpads(x, _):
        for b in (ch, ck):
            b[x, 0:8, :] = zc
            b[x, 72:80, :] = zc
        return 0

    lax.fori_loop(0, 8, cpads, 0)
    pi = lax.broadcasted_iota(jnp.int32, (256, 128), 0)
    pj = lax.broadcasted_iota(jnp.int32, (256, 128), 1)
    pick[...] = jnp.where(pi // 2 == pj, 0.125, 0.0).astype(jnp.bfloat16)

    @pl.when(d == last)
    def _():
        def zero(i, _):
            hb[16, pl.ds(TOP + i * 8, 8), :] = z8
            kb[16, pl.ds(TOP + i * 8, 8), :] = z8
            return 0

        lax.fori_loop(0, 16, zero, 0)

        def czero(i, _):
            ch[8, pl.ds(8 + i * 8, 8), :] = zc
            ck[8, pl.ds(8 + i * 8, 8), :] = zc
            return 0

        lax.fori_loop(0, 8, czero, 0)

    def remote(src, dst, ssem, rsem, g2, d2):
        return pltpu.make_async_remote_copy(src_ref=src, dst_ref=dst, send_sem=ssem, recv_sem=rsem,
                                            device_id=(g2, d2), device_id_type=MESH)

    down = d - 1
    upper = d + 1

    def part(i, first):
        return pl.ds(first + i * (128 // NH), 128 // NH)

    halo_h = [remote(hb.at[0, part(i, TOP), :], hb.at[16, part(i, TOP), :], halo_s.at[i], halo_r.at[i], g, down) for i in range(NH)]
    halo_k = [remote(kb.at[0, part(i, TOP), :], kb.at[16, part(i, TOP), :], halo_s.at[NH + i], halo_r.at[NH + i], g, down)
              for i in range(NH)]
    halo_f = [remote(f15.at[part(i, 0), :], frecv.at[part(i, 0), :], halo_s.at[2 * NH + i], halo_r.at[2 * NH + i], g, upper)
              for i in range(NH)]
    crow = pl.ds(8, 64)
    chalo_h = remote(ch.at[0, crow, :], ch.at[8, crow, :], halo_s.at[3 * NH], halo_r.at[3 * NH], g, down)
    chalo_k = remote(ck.at[0, crow, :], ck.at[8, crow, :], halo_s.at[3 * NH + 1], halo_r.at[3 * NH + 1], g, down)
    chalo_f = remote(cf7, cfrecv, halo_s.at[3 * NH + 2], halo_r.at[3 * NH + 2], g, upper)

    def on(condition, act):
        pl.when(condition)(act)

    def chunks(act, first=0, rows=128):
        def body(i, _):
            act(pl.multiple_of(first + i * CH, CH))
            return 0

        lax.fori_loop(0, rows // CH, body, 0)

    def halo_start():
        def act():
            for i in range(NH):
                halo_h[i].start()
                halo_k[i].start()

        on(d > 0, act)

    def restrict(a, b, store):
        for r in range(0, 128, CH):
            s = a(r) + b(r)
            for q in range(4):
                vs[q, r : r + CH, :] = s[:, q * 128 : (q + 1) * 128]
        for half in range(2):
            parts = [vs[q, pl.ds(0, 64, 2), :] + vs[q, pl.ds(1, 64, 2), :] for q in (2 * half, 2 * half + 1)]
            e = jnp.concatenate(parts, axis=1)
            hi = e.astype(jnp.bfloat16)
            lo = (e - hi.astype(F32)).astype(jnp.bfloat16)
            w = pick[...]
            o = jnp.dot(hi, w, preferred_element_type=F32) + jnp.dot(lo, w, preferred_element_type=F32)
            store(half, o)

    def into(buf, pos):
        def store(half, o):
            buf[:, pos, :, half * 128 : (half + 1) * 128] = o.reshape(8, 8, 128)

        return store

    def a_copies(p):
        return [remote(p.buf.at[mate(s)[0]], p.ab.at[me], p.a_s.at[s - 1], p.a_r.at[s - 1], mate(s)[1], d) for s in range(1, NP)]

    def a_start(p):
        for c in a_copies(p):
            c.start()
        p.ab[me] = p.buf[me]

    def b_copy(p):
        return remote(p.x, p.y, cross_s.at[p.i], cross_r.at[p.i], other, d)

    def b_start(p):
        for c in a_copies(p):
            c.wait()
        for n in range(cap):
            p.x[n] = p.ab[cross[n]]
        b_copy(p).start()

    def c_copies(p):
        return [remote(p.c.at[mate(s)[0]], p.to.at[me], p.c_s.at[s - 1], p.c_r.at[s - 1], mate(s)[1], d) for s in range(1, NP)]

    def c_start(p):
        b_copy(p).wait()
        for j in range(NP):
            mine, slot, crossed = where[j]
            p.c[j] = jnp.where(mine, p.ab[slot], p.y[crossed])
        for c in c_copies(p):
            c.start()
        p.to[me] = p.c[me]

    def c_wait(p):
        for c in c_copies(p):
            c.wait()

    start = Payload(0, sbuf, sab, sx, sy, sc, sd, sa_s, sa_r, sc_s, sc_r)
    second = Payload(3, tbuf, tab, tx, ty, tc, td, ta_s, ta_r, tc_s, tc_r)
    inner = Payload(1, nbuf, nab, nx, ny, nc, nd, na_s, na_r, nc_s, nc_r)
    more = Payload(4, mbuf, mab, mx, my, mc, md, ma_s, ma_r, mc_s, mc_r)
    outer = Payload(2, bbuf, bab, bx, by, bc, bd, ba_s, ba_r, bc_s, bc_r)

    def spot(l):
        return (start, FIRST.index(l)) if l in FIRST else (second, SECOND.index(l))

    def start_small(l):
        if l:
            hload(l).wait()
        p, pos = spot(l)
        restrict(lambda r: hb[2 * l, pl.ds(TOP + r, CH), :], lambda r: hb[2 * l + 1, pl.ds(TOP + r, CH), :], into(p.buf, pos))

    def close(x):
        def act(r):
            k, w = closure(hb[x, pl.ds(TOP + r, CH), :], kb[x, pl.ds(TOP + r, CH), :], 1.0)
            kb[x, pl.ds(TOP + r, CH), :] = k
            wb[x, pl.ds(r, CH), :] = w

        chunks(act)

    def face(x, r):
        here, there = (x, pl.ds(TOP + r, CH), slice(None)), (x + 1, pl.ds(TOP + r, CH), slice(None))
        return (kb[there] + kb[here]) * (hb[there] - hb[here])

    def first_face():
        def act(r):
            f = face(0, r)
            f01[pl.ds(r, CH), :] = f
            fx[pl.ds(r, CH), :] = f

        chunks(act)

    def step(x):
        def act(r):
            h, k, tot = in_layer(hb, kb, x, r, CH, 1.0)
            f = (kb[x + 1, pl.ds(TOP + r, CH), :] + k) * (hb[x + 1, pl.ds(TOP + r, CH), :] - h)
            tot = tot + (f - fx[pl.ds(r, CH), :])
            fx[pl.ds(r, CH), :] = f
            wb[x, pl.ds(r, CH), :] = h + tot * wb[x, pl.ds(r, CH), :]

        chunks(act)

    def step_between(x, above, below):
        def act(r):
            h, k, tot = in_layer(hb, kb, x, r, CH, 1.0)
            tot = tot + (above[pl.ds(r, CH), :] - below[pl.ds(r, CH), :])
            wb[x, pl.ds(r, CH), :] = h + tot * wb[x, pl.ds(r, CH), :]

        chunks(act)

    def upper_face(i):
        def arrived():
            halo_h[i].wait_recv()
            halo_k[i].wait_recv()

        on(d < last, arrived)

        def act(r):
            f15[pl.ds(r, CH), :] = face(15, r)

        chunks(act, i * (128 // NH), 128 // NH)
        on(d < last, halo_f[i].start)

    def lower_face():
        def arrived():
            for c in halo_f:
                c.wait_recv()

        on(d > 0, arrived)

        def edge():
            def act(r):
                frecv[pl.ds(r, CH), :] = hb[0, pl.ds(TOP + r, CH), :] * kb[0, pl.ds(TOP + r, CH), :]

            chunks(act)

        on(d == 0, edge)

    def out_pair(l):
        return load(wb.at[pl.ds(2 * l, 2)], fine_out.at[0, pl.ds(2 * l, 2)], osem.at[l])

    def next_small(l, buf, pos):
        restrict(lambda r: wb[2 * l, pl.ds(r, CH), :], lambda r: wb[2 * l + 1, pl.ds(r, CH), :], into(buf, pos))
        out_pair(l).start()

    def close_coarse(l):
        p, pos = spot(l)
        h = p.to[:, pos].reshape(64, 256)
        k, w = closure(h, ck[l, crow, :], 2.0)
        ch[l, crow, :] = h
        ck[l, crow, :] = k
        cw[l] = w

    def chalo_start():
        def act():
            chalo_h.start()
            chalo_k.start()

        on(d > 0, act)

    def cface(x):
        return (ck[x + 1, crow, :] + ck[x, crow, :]) * (ch[x + 1, crow, :] - ch[x, crow, :])

    def first_cface():
        f = cface(0)
        cf01[...] = f
        cfx[...] = f

    def step_coarse(x):
        h, k, tot = in_layer(ch, ck, x, 0, 64, 2.0)
        f = cface(x)
        tot = tot + (f - cfx[...])
        cfx[...] = f
        cw[x] = h + tot * cw[x]

    def step_coarse_between(x, above, below):
        h, k, tot = in_layer(ch, ck, x, 0, 64, 2.0)
        cw[x] = h + (tot + (above[...] - below[...])) * cw[x]

    def upper_cface():
        def arrived():
            chalo_h.wait_recv()
            chalo_k.wait_recv()

        on(d < last, arrived)
        cf7[...] = cface(7)
        on(d < last, chalo_f.start)

    def lower_cface():
        on(d > 0, chalo_f.wait_recv)

        def edge():
            cfrecv[...] = ch[0, crow, :] * ck[0, crow, :]

        on(d == 0, edge)

    cout = load(cw, coarse_out.at[0], csem)

    def difference(l, to, pos):
        dbuf[l] = to[:, pos].reshape(64, 256) - cw[l]

    def pair(l):
        if l < 6:
            kload(l + 1).wait()
        close(2 * l + 1)
        close(2 * l + 2)
        step(2 * l)
        step(2 * l + 1)
        next_small(l, nbuf if l < 4 else mbuf, (l - 1) % 3)

    def down_sent():
        for c in halo_h + halo_k:
            c.wait_send()
        chalo_h.wait_send()
        chalo_k.wait_send()

    def up_sent():
        for c in halo_f:
            c.wait_send()
        chalo_f.wait_send()

    hload(0).wait()
    kload(0).wait()
    close(0)
    pload.wait()
    cross = [jnp.int32(0)] * cap
    count = jnp.int32(0)
    for j in range(NP):
        p = pairing[index_of(j, 1 - zh)]
        mine = lax.rem(p // 2, 2) == zh
        slot = (p // 4) * 2 + lax.rem(p, 2)
        for i in range(cap):
            cross[i] = jnp.where(mine & (count == i), slot, cross[i])
        count = count + jnp.where(mine, 1, 0)
    where = []
    count = jnp.int32(0)
    for j in range(NP):
        p = pairing[index_of(j, zh)]
        mine = lax.rem(p // 2, 2) == zh
        where.append((mine, (p // 4) * 2 + lax.rem(p, 2), jnp.minimum(count, cap - 1)))
        count = count + jnp.where(mine, 0, 1)

    for l in FIRST[:1]:
        start_small(l)
    pl.semaphore_wait(bar, NP + jnp.where(d > 0, 1, 0) + jnp.where(d < last, 1, 0))
    halo_start()
    for l in FIRST[1:]:
        start_small(l)
    a_start(start)
    for l in SECOND:
        start_small(l)
    a_start(second)
    close(1)
    first_face()
    kload(7).wait()
    close(15)
    kload(1).wait()
    close(2)
    step(1)
    pair(1)
    pair(2)
    pair(3)
    a_start(inner)
    b_start(start)
    upper_face(0)
    pair(4)
    b_start(second)
    pair(5)
    pair(6)
    a_start(more)
    b_start(inner)
    c_start(start)
    upper_face(1)
    step(14)
    c_start(second)
    step_between(15, f15, fx)
    next_small(7, bbuf, 1)
    c_wait(start)
    cload.wait()
    for l in FIRST:
        close_coarse(l)
    chalo_start()
    b_start(more)
    c_start(inner)
    lower_face()
    step_between(0, f01, frecv)
    next_small(0, bbuf, 0)
    a_start(outer)
    c_wait(second)
    for l in SECOND:
        close_coarse(l)
    first_cface()
    for x in range(1, 7):
        step_coarse(x)
    b_start(outer)
    upper_cface()
    step_coarse_between(7, cf7, cfx)
    c_wait(inner)
    for l in range(1, 4):
        difference(l, nd, l - 1)
    c_start(more)
    c_start(outer)
    lower_cface()
    step_coarse_between(0, cf01, cfrecv)
    cout.start()
    c_wait(more)
    for l in range(4, 7):
        difference(l, md, l - 4)
    dout = [
        load(dbuf.at[pl.ds(1, 6)], diff_out.at[0, pl.ds(1, 6)], ksem.at[0]),
        load(dbuf.at[0], diff_out.at[0, 0], ksem.at[1]),
        load(dbuf.at[7], diff_out.at[0, 7], ksem.at[2]),
    ]
    dout[0].start()
    for l in range(8):
        out_pair(l).wait()
    cout.wait()
    on(d > 0, down_sent)
    on(d < last, up_sent)
    c_wait(outer)
    difference(0, bd, 0)
    dout[1].start()
    difference(7, bd, 1)
    dout[2].start()
    for c in dout:
        c.wait()


class Payload:
    def __init__(self, i, buf, ab, x, y, c, to, a_s, a_r, c_s, c_r):
        self.i, self.buf, self.ab, self.x, self.y, self.c, self.to = i, buf, ab, x, y, c, to
        self.a_s, self.a_r, self.c_s, self.c_r = a_s, a_r, c_s, c_r


def payload(cap, layers):
    piece = (layers, 8, 256)
    return [
        pltpu.VMEM((NP,) + piece, F32),
        pltpu.VMEM((NP,) + piece, F32),
        pltpu.VMEM((cap,) + piece, F32),
        pltpu.VMEM((cap,) + piece, F32),
        pltpu.VMEM((NP,) + piece, F32),
        pltpu.VMEM((NP,) + piece, F32),
    ]


def run(cap, pairing, head, cond, ccond):
    dma = pltpu.SemaphoreType.DMA
    scratch = [
        pltpu.VMEM((17, 144, 512), F32),
        pltpu.VMEM((17, 144, 512), F32),
        pltpu.VMEM((16, 128, 512), F32),
        *[pltpu.VMEM((128, 512), F32)] * 4,
        pltpu.VMEM((4, 128, 128), F32),
        pltpu.VMEM((256, 128), jnp.bfloat16),
        pltpu.SMEM((16,), jnp.int32),
        *payload(cap, 4),
        *payload(cap, 4),
        *payload(cap, 3),
        *payload(cap, 3),
        *payload(cap, 2),
        pltpu.VMEM((9, 80, 256), F32),
        pltpu.VMEM((9, 80, 256), F32),
        pltpu.VMEM((8, 64, 256), F32),
        *[pltpu.VMEM((64, 256), F32)] * 4,
        pltpu.VMEM((8, 64, 256), F32),
        dma((8,)), dma((8,)), dma, dma((8,)), dma((3 * NH + 3,)), dma((3 * NH + 3,)),
        *[dma((NP - 1,))] * 20,
        dma((5,)), dma((5,)), dma,
    ]
    anywhere = pl.BlockSpec(memory_space=pl.ANY)
    return pl.pallas_call(
        functools.partial(kernel, cap),
        out_shape=(
            jax.ShapeDtypeStruct(head.shape, F32),
            jax.ShapeDtypeStruct(ccond.shape, F32),
            jax.ShapeDtypeStruct(ccond.shape, F32),
        ),
        in_specs=[pl.BlockSpec(memory_space=pltpu.HBM)] * 4,
        out_specs=(anywhere, anywhere, anywhere),
        scratch_shapes=scratch,
        compiler_params=pltpu.CompilerParams(
            collective_id=cap, has_side_effects=True, vmem_limit_bytes=48 * 2**20
        ),
    )(*[pltpu.with_memory_space_constraint(v, pltpu.HBM) for v in (pairing, head, cond, ccond)])


def write_out(fine, coarse, diff, fine_out, coarse_out, diff_out, sem):
    copies = [pltpu.make_async_copy(fine.at[0, pl.ds(4 * i, 4)], fine_out.at[0, pl.ds(4 * i, 4)], sem.at[i]) for i in range(4)]
    copies.append(pltpu.make_async_copy(coarse, coarse_out, sem.at[4]))
    copies.append(pltpu.make_async_copy(diff, diff_out, sem.at[5]))
    for c in copies:
        c.start()
    for c in copies:
        c.wait()


def finish(*results):
    anywhere = pl.BlockSpec(memory_space=pl.ANY)
    return pl.pallas_call(
        write_out,
        out_shape=tuple(pltpu.HBM(r.shape, r.dtype) for r in results),
        in_specs=[anywhere] * 3,
        out_specs=(anywhere,) * 3,
        scratch_shapes=[pltpu.SemaphoreType.DMA((6,))],
        compiler_params=pltpu.CompilerParams(vmem_limit_bytes=2**20),
    )(*[pltpu.with_memory_space_constraint(r, pltpu.VMEM) for r in results])


def whole(cap, *arrays):
    return finish(*run(cap, *arrays))


def per_device(head, conductivity, coarse_conductivity, pairing):
    i = jnp.arange(16)
    crossing = jnp.where((i // 2) % 2 == 0, (pairing // 2) % 2, 0) - jnp.where(i == 0, CAPS[0], 0)
    kernels = [functools.partial(whole, cap) for cap in CAPS]
    return lax.switch(jnp.sum(crossing), kernels, pairing, head, conductivity, coarse_conductivity)


def solution(mesh):
    block = P("group", "dom", None, None)
    return jax.shard_map(
        per_device,
        mesh=mesh,
        in_specs=(block, block, block, P()),
        out_specs=(block, block, block),
        check_vma=False,
    )
```

```python
import functools

import jax
import jax.numpy as jnp
from jax import lax
from jax.experimental import pallas as pl
from jax.experimental.pallas import tpu as pltpu
from jax.sharding import PartitionSpec as P

MESH = pl.DeviceIdType.MESH
F32 = jnp.float32
NP = 8
CAPS = (3, 4, 5, 6, 8)

TOP = 8
CH = 32
NH = 2


FIRST = (0, 7, 1, 2)
SECOND = (3, 4, 5, 6)


def closure(h, cond, spacing):
    t = 1.5 * jnp.minimum(h, 0.0)
    r = lax.rsqrt(1.0 + t * t)
    p = t * r
    a = 1.0 + p
    k = cond * (r * lax.rsqrt(r) * (a * a))
    s2 = spacing * spacing
    w = 1.0 / (20.0 * s2 - (24.0 * s2) * (p * (r * r)))
    return k, w


def in_layer(hb, kb, x, row, rows, spacing):
    ha = hb[x, pl.ds(row, rows + 16), :]
    ka = kb[x, pl.ds(row, rows + 16), :]
    h, k = ha[8 : 8 + rows], ka[8 : 8 + rows]
    tot = (ka[9 : 9 + rows] + k) * (ha[9 : 9 + rows] - h)
    hd, kd = ha[7 : 7 + rows], ka[7 : 7 + rows]
    tot = tot + (kd + k) * (hd - h)
    n = h.shape[1]
    lane = lax.broadcasted_iota(jnp.int32, h.shape, 1)
    hz = jnp.where(lane == n - 1, 0.0, pltpu.roll(h, n - 1, 1))
    kz = jnp.where(lane == n - 1, 0.0, pltpu.roll(k, n - 1, 1))
    hs = h - spacing
    fz = (kz + k) * (hz - hs)
    fd = jnp.where(lane == 0, k * (h + spacing), pltpu.roll(fz, 1, 1))
    return h, k, tot + (fz - fd)


def kernel(cap, pairing_in, head, cond, ccond, fine_out, coarse_out, diff_out,
           hb, kb, fx, f01, f15, frecv, vs, pick, pairing,
           sbuf, sab, sx, sy, sc, sd, tbuf, tab, tx, ty, tc, td, nbuf, nab, nx, ny, nc, nd, mbuf, mab, mx, my, mc, md, bbuf, bab, bx, by, bc, bd,
           ch, ck, cfx, cf01, cf7, cfrecv,
           hsem, ksem, csem, halo_s, halo_r, sa_s, sa_r, ta_s, ta_r, na_s, na_r, ma_s, ma_r, ba_s, ba_r, sc_s, sc_r, tc_s, tc_r, nc_s, nc_r, mc_s, mc_r, bc_s, bc_r,
           cross_s, cross_r, psem):
    wb, cw, dbuf = fine_out.at[0], coarse_out.at[0], diff_out.at[0]
    g = lax.axis_index("group")
    d = lax.axis_index("dom")
    zh = lax.rem(g // 2, 2)
    me = (g // 4) * 2 + lax.rem(g, 2)

    def index_of(j, plane):
        return (j // 2) * 4 + plane * 2 + lax.rem(j, 2)

    def mate(s):
        j = lax.rem(me + s, NP)
        return j, index_of(j, zh)

    other = index_of(me, 1 - zh)
    last = 7

    def load(src, dst, sem):
        return pltpu.make_async_copy(src, dst, sem)

    def hload(l):
        return load(head.at[0, pl.ds(2 * l, 2)], hb.at[pl.ds(2 * l, 2), pl.ds(TOP, 128), :], hsem.at[l])

    def kload(l):
        return load(cond.at[0, pl.ds(2 * l, 2)], kb.at[pl.ds(2 * l, 2), pl.ds(TOP, 128), :], ksem.at[l])

    cload = load(ccond.at[0], ck.at[pl.ds(0, 8), pl.ds(8, 64), :], csem)
    bar = pltpu.get_barrier_semaphore()

    def greet(g2, d2):
        pl.semaphore_signal(bar, inc=1, device_id=(g2, d2), device_id_type=MESH)

    for s in range(1, NP):
        greet(mate(s)[1], d)
    greet(other, d)

    @pl.when(d > 0)
    def _():
        greet(g, d - 1)

    @pl.when(d < last)
    def _():
        greet(g, d + 1)

    pload = load(pairing_in, pairing, psem)
    hload(0).start()
    kload(0).start()
    pload.start()
    for l in range(1, 8):
        hload(l).start()
    for l in range(1, 8):
        kload(l).start()
    cload.start()

    def remote(src, dst, ssem, rsem, g2, d2):
        return pltpu.make_async_remote_copy(src_ref=src, dst_ref=dst, send_sem=ssem, recv_sem=rsem,
                                            device_id=(g2, d2), device_id_type=MESH)

    down = d - 1
    upper = d + 1

    def part(i, first):
        return pl.ds(first + i * (128 // NH), 128 // NH)

    halo_h = [remote(hb.at[0, part(i, TOP), :], hb.at[16, part(i, TOP), :], halo_s.at[i], halo_r.at[i], g, down) for i in range(NH)]
    halo_k = [remote(kb.at[0, part(i, TOP), :], kb.at[16, part(i, TOP), :], halo_s.at[NH + i], halo_r.at[NH + i], g, down)
              for i in range(NH)]
    halo_f = [remote(f15.at[part(i, 0), :], frecv.at[part(i, 0), :], halo_s.at[2 * NH + i], halo_r.at[2 * NH + i], g, upper)
              for i in range(NH)]
    crow = pl.ds(8, 64)
    chalo_h = remote(ch.at[0, crow, :], ch.at[8, crow, :], halo_s.at[3 * NH], halo_r.at[3 * NH], g, down)
    chalo_k = remote(ck.at[0, crow, :], ck.at[8, crow, :], halo_s.at[3 * NH + 1], halo_r.at[3 * NH + 1], g, down)
    chalo_f = remote(cf7, cfrecv, halo_s.at[3 * NH + 2], halo_r.at[3 * NH + 2], g, upper)

    def on(condition, act):
        pl.when(condition)(act)

    def chunks(act, first=0, rows=128):
        def body(i, _):
            act(pl.multiple_of(first + i * CH, CH))
            return 0

        lax.fori_loop(0, rows // CH, body, 0)

    def halo_start():
        def act():
            for i in range(NH):
                halo_h[i].start()
                halo_k[i].start()

        on(d > 0, act)

    def restrict(a, b, store):
        for r in range(0, 128, CH):
            s = a(r) + b(r)
            for q in range(4):
                vs[q, r : r + CH, :] = s[:, q * 128 : (q + 1) * 128]
        for half in range(2):
            parts = [vs[q, pl.ds(0, 64, 2), :] + vs[q, pl.ds(1, 64, 2), :] for q in (2 * half, 2 * half + 1)]
            e = jnp.concatenate(parts, axis=1)
            hi = e.astype(jnp.bfloat16)
            lo = (e - hi.astype(F32)).astype(jnp.bfloat16)
            w = pick[...]
            o = jnp.dot(hi, w, preferred_element_type=F32) + jnp.dot(lo, w, preferred_element_type=F32)
            store(half, o)

    def into(buf, pos):
        def store(half, o):
            buf[:, pos, :, half * 128 : (half + 1) * 128] = o.reshape(8, 8, 128)

        return store

    def scatter(buf, to, ssem, rsem):
        for s in range(1, NP):
            j, g2 = mate(s)
            remote(buf.at[j], to.at[me], ssem, rsem, g2, d).start()
        to[me] = buf[me]

    def scattered(buf, to, ssem, rsem):
        most = pl.ds(0, NP - 1)
        remote(buf.at[most], to.at[most], ssem, rsem, mate(1)[1], d).wait()

    def a_start(p):
        scatter(p.buf, p.ab, p.a_s, p.a_r)

    def b_copy(p):
        return remote(p.x, p.y, cross_s.at[p.i], cross_r.at[p.i], other, d)

    def b_start(p):
        scattered(p.buf, p.ab, p.a_s, p.a_r)
        for n in range(cap):
            p.x[n] = p.ab[cross[n]]
        b_copy(p).start()

    def c_start(p):
        b_copy(p).wait()
        for j in range(NP):
            mine, slot, crossed = where[j]
            p.c[j] = jnp.where(mine, p.ab[slot], p.y[crossed])
        scatter(p.c, p.to, p.c_s, p.c_r)

    def c_wait(p):
        scattered(p.c, p.to, p.c_s, p.c_r)

    start = Payload(0, sbuf, sab, sx, sy, sc, sd, sa_s, sa_r, sc_s, sc_r)
    second = Payload(3, tbuf, tab, tx, ty, tc, td, ta_s, ta_r, tc_s, tc_r)
    inner = Payload(1, nbuf, nab, nx, ny, nc, nd, na_s, na_r, nc_s, nc_r)
    more = Payload(4, mbuf, mab, mx, my, mc, md, ma_s, ma_r, mc_s, mc_r)
    outer = Payload(2, bbuf, bab, bx, by, bc, bd, ba_s, ba_r, bc_s, bc_r)

    def spot(l):
        return (start, FIRST.index(l)) if l in FIRST else (second, SECOND.index(l))

    def start_small(l):
        if l:
            hload(l).wait()
        p, pos = spot(l)
        restrict(lambda r: hb[2 * l, pl.ds(TOP + r, CH), :], lambda r: hb[2 * l + 1, pl.ds(TOP + r, CH), :], into(p.buf, pos))

    def close(x):
        def act(r):
            k, w = closure(hb[x, pl.ds(TOP + r, CH), :], kb[x, pl.ds(TOP + r, CH), :], 1.0)
            kb[x, pl.ds(TOP + r, CH), :] = k
            wb[x, pl.ds(r, CH), :] = w

        chunks(act)

    def face(x, r):
        here, there = (x, pl.ds(TOP + r, CH), slice(None)), (x + 1, pl.ds(TOP + r, CH), slice(None))
        return (kb[there] + kb[here]) * (hb[there] - hb[here])

    def first_face():
        def act(r):
            f = face(0, r)
            f01[pl.ds(r, CH), :] = f
            fx[pl.ds(r, CH), :] = f

        chunks(act)

    def step(x):
        def act(r):
            h, k, tot = in_layer(hb, kb, x, r, CH, 1.0)
            f = (kb[x + 1, pl.ds(TOP + r, CH), :] + k) * (hb[x + 1, pl.ds(TOP + r, CH), :] - h)
            tot = tot + (f - fx[pl.ds(r, CH), :])
            fx[pl.ds(r, CH), :] = f
            wb[x, pl.ds(r, CH), :] = h + tot * wb[x, pl.ds(r, CH), :]

        chunks(act)

    def step_between(x, above, below):
        def act(r):
            h, k, tot = in_layer(hb, kb, x, r, CH, 1.0)
            tot = tot + (above[pl.ds(r, CH), :] - below[pl.ds(r, CH), :])
            wb[x, pl.ds(r, CH), :] = h + tot * wb[x, pl.ds(r, CH), :]

        chunks(act)

    def upper_face(i):
        def arrived():
            halo_h[i].wait_recv()
            halo_k[i].wait_recv()

        on(d < last, arrived)

        def act(r):
            f15[pl.ds(r, CH), :] = face(15, r)

        chunks(act, i * (128 // NH), 128 // NH)
        on(d < last, halo_f[i].start)

    def lower_face():
        def arrived():
            for c in halo_f:
                c.wait_recv()

        on(d > 0, arrived)

        def edge():
            def act(r):
                frecv[pl.ds(r, CH), :] = hb[0, pl.ds(TOP + r, CH), :] * kb[0, pl.ds(TOP + r, CH), :]

            chunks(act)

        on(d == 0, edge)

    def next_small(l, buf, pos):
        restrict(lambda r: wb[2 * l, pl.ds(r, CH), :], lambda r: wb[2 * l + 1, pl.ds(r, CH), :], into(buf, pos))

    def close_coarse(l):
        p, pos = spot(l)
        h = p.to[:, pos].reshape(64, 256)
        k, w = closure(h, ck[l, crow, :], 2.0)
        ch[l, crow, :] = h
        ck[l, crow, :] = k
        cw[l] = w

    def chalo_start():
        def act():
            chalo_h.start()
            chalo_k.start()

        on(d > 0, act)

    def cface(x):
        return (ck[x + 1, crow, :] + ck[x, crow, :]) * (ch[x + 1, crow, :] - ch[x, crow, :])

    def first_cface():
        f = cface(0)
        cf01[...] = f
        cfx[...] = f

    def step_coarse(x):
        h, k, tot = in_layer(ch, ck, x, 0, 64, 2.0)
        f = cface(x)
        tot = tot + (f - cfx[...])
        cfx[...] = f
        cw[x] = h + tot * cw[x]

    def step_coarse_between(x, above, below):
        h, k, tot = in_layer(ch, ck, x, 0, 64, 2.0)
        cw[x] = h + (tot + (above[...] - below[...])) * cw[x]

    def upper_cface():
        def arrived():
            chalo_h.wait_recv()
            chalo_k.wait_recv()

        on(d < last, arrived)
        cf7[...] = cface(7)
        on(d < last, chalo_f.start)

    def lower_cface():
        on(d > 0, chalo_f.wait_recv)

        def edge():
            cfrecv[...] = ch[0, crow, :] * ck[0, crow, :]

        on(d == 0, edge)

    def difference(l, to, pos):
        dbuf[l] = to[:, pos].reshape(64, 256) - cw[l]

    def pair(l):
        if l < 6:
            kload(l + 1).wait()
        close(2 * l + 1)
        close(2 * l + 2)
        step(2 * l)
        step(2 * l + 1)
        next_small(l, nbuf if l < 4 else mbuf, (l - 1) % 3)

    def down_sent():
        for c in halo_h + halo_k:
            c.wait_send()
        chalo_h.wait_send()
        chalo_k.wait_send()

    def up_sent():
        for c in halo_f:
            c.wait_send()
        chalo_f.wait_send()

    hload(0).wait()
    kload(0).wait()
    close(0)
    pload.wait()
    cross = [jnp.int32(0)] * cap
    count = jnp.int32(0)
    for j in range(NP):
        p = pairing[index_of(j, 1 - zh)]
        mine = lax.rem(p // 2, 2) == zh
        slot = (p // 4) * 2 + lax.rem(p, 2)
        for i in range(cap):
            cross[i] = jnp.where(mine & (count == i), slot, cross[i])
        count = count + jnp.where(mine, 1, 0)
    where = []
    count = jnp.int32(0)
    for j in range(NP):
        p = pairing[index_of(j, zh)]
        mine = lax.rem(p // 2, 2) == zh
        where.append((mine, (p // 4) * 2 + lax.rem(p, 2), jnp.minimum(count, cap - 1)))
        count = count + jnp.where(mine, 0, 1)

    pi = lax.broadcasted_iota(jnp.int32, (256, 128), 0)
    pj = lax.broadcasted_iota(jnp.int32, (256, 128), 1)
    pick[...] = jnp.where(pi // 2 == pj, 0.125, 0.0).astype(jnp.bfloat16)

    for l in FIRST[:1]:
        start_small(l)
    pl.semaphore_wait(bar, NP + jnp.where(d > 0, 1, 0) + jnp.where(d < last, 1, 0))
    halo_start()
    z8 = jnp.zeros((8, 512), F32)
    zc = jnp.zeros((8, 256), F32)

    def pads(x, _):
        for b in (hb, kb):
            b[x, 0:8, :] = z8
            b[x, 136:144, :] = z8
        return 0

    lax.fori_loop(0, 16, pads, 0)

    def cpads(x, _):
        for b in (ch, ck):
            b[x, 0:8, :] = zc
            b[x, 72:80, :] = zc
        return 0

    lax.fori_loop(0, 8, cpads, 0)
    @pl.when(d == last)
    def _():
        def zero(i, _):
            hb[16, pl.ds(TOP + i * 8, 8), :] = z8
            kb[16, pl.ds(TOP + i * 8, 8), :] = z8
            return 0

        lax.fori_loop(0, 16, zero, 0)

        def czero(i, _):
            ch[8, pl.ds(8 + i * 8, 8), :] = zc
            ck[8, pl.ds(8 + i * 8, 8), :] = zc
            return 0

        lax.fori_loop(0, 8, czero, 0)

    for l in FIRST[1:]:
        start_small(l)
    a_start(start)
    for l in SECOND:
        start_small(l)
    a_start(second)
    close(1)
    first_face()
    kload(7).wait()
    close(15)
    kload(1).wait()
    close(2)
    step(1)
    pair(1)
    pair(2)
    pair(3)
    a_start(inner)
    b_start(start)
    upper_face(0)
    pair(4)
    b_start(second)
    pair(5)
    pair(6)
    a_start(more)
    b_start(inner)
    c_start(start)
    upper_face(1)
    step(14)
    c_start(second)
    step_between(15, f15, fx)
    next_small(7, bbuf, 1)
    c_wait(start)
    cload.wait()
    for l in FIRST:
        close_coarse(l)
    chalo_start()
    b_start(more)
    c_start(inner)
    lower_face()
    step_between(0, f01, frecv)
    next_small(0, bbuf, 0)
    a_start(outer)
    c_wait(second)
    for l in SECOND:
        close_coarse(l)
    first_cface()
    for x in range(1, 7):
        step_coarse(x)
    b_start(outer)
    upper_cface()
    step_coarse_between(7, cf7, cfx)
    c_wait(inner)
    for l in range(1, 4):
        difference(l, nd, l - 1)
    c_start(more)
    c_start(outer)
    lower_cface()
    step_coarse_between(0, cf01, cfrecv)
    c_wait(more)
    for l in range(4, 7):
        difference(l, md, l - 4)
    on(d > 0, down_sent)
    on(d < last, up_sent)
    c_wait(outer)
    difference(0, bd, 0)
    difference(7, bd, 1)


class Payload:
    def __init__(self, i, buf, ab, x, y, c, to, a_s, a_r, c_s, c_r):
        self.i, self.buf, self.ab, self.x, self.y, self.c, self.to = i, buf, ab, x, y, c, to
        self.a_s, self.a_r, self.c_s, self.c_r = a_s, a_r, c_s, c_r


def payload(cap, layers):
    piece = (layers, 8, 256)
    return [
        pltpu.VMEM((NP,) + piece, F32),
        pltpu.VMEM((NP,) + piece, F32),
        pltpu.VMEM((cap,) + piece, F32),
        pltpu.VMEM((cap,) + piece, F32),
        pltpu.VMEM((NP,) + piece, F32),
        pltpu.VMEM((NP,) + piece, F32),
    ]


def run(cap, pairing, head, cond, ccond):
    dma = pltpu.SemaphoreType.DMA
    scratch = [
        pltpu.VMEM((17, 144, 512), F32),
        pltpu.VMEM((17, 144, 512), F32),
        *[pltpu.VMEM((128, 512), F32)] * 4,
        pltpu.VMEM((4, 128, 128), F32),
        pltpu.VMEM((256, 128), jnp.bfloat16),
        pltpu.SMEM((16,), jnp.int32),
        *payload(cap, 4),
        *payload(cap, 4),
        *payload(cap, 3),
        *payload(cap, 3),
        *payload(cap, 2),
        pltpu.VMEM((9, 80, 256), F32),
        pltpu.VMEM((9, 80, 256), F32),
        *[pltpu.VMEM((64, 256), F32)] * 4,
        dma((8,)), dma((8,)), dma, dma((3 * NH + 3,)), dma((3 * NH + 3,)),
        *[dma] * 20,
        dma((5,)), dma((5,)), dma,
    ]
    return pl.pallas_call(
        functools.partial(kernel, cap),
        out_shape=(pltpu.VMEM(head.shape, F32), pltpu.VMEM(ccond.shape, F32), pltpu.VMEM(ccond.shape, F32)),
        in_specs=[pl.BlockSpec(memory_space=pltpu.HBM)] * 4,
        out_specs=(pl.BlockSpec(memory_space=pltpu.VMEM),) * 3,
        scratch_shapes=scratch,
        compiler_params=pltpu.CompilerParams(
            collective_id=cap, has_side_effects=True, vmem_limit_bytes=48 * 2**20
        ),
    )(*[pltpu.with_memory_space_constraint(v, pltpu.HBM) for v in (pairing, head, cond, ccond)])


def write_out(fine, coarse, diff, fine_out, coarse_out, diff_out, sem):
    copies = [pltpu.make_async_copy(fine.at[0, pl.ds(4 * i, 4)], fine_out.at[0, pl.ds(4 * i, 4)], sem.at[i]) for i in range(4)]
    copies.append(pltpu.make_async_copy(coarse, coarse_out, sem.at[4]))
    copies.append(pltpu.make_async_copy(diff, diff_out, sem.at[5]))
    for c in copies:
        c.start()
    for c in copies:
        c.wait()


def finish(*results):
    anywhere = pl.BlockSpec(memory_space=pl.ANY)
    return pl.pallas_call(
        write_out,
        out_shape=tuple(pltpu.HBM(r.shape, r.dtype) for r in results),
        in_specs=[anywhere] * 3,
        out_specs=(anywhere,) * 3,
        scratch_shapes=[pltpu.SemaphoreType.DMA((6,))],
        compiler_params=pltpu.CompilerParams(vmem_limit_bytes=2**20),
    )(*[pltpu.with_memory_space_constraint(r, pltpu.VMEM) for r in results])


def whole(cap, *arrays):
    return finish(*run(cap, *arrays))


def per_device(head, conductivity, coarse_conductivity, pairing):
    i = jnp.arange(16)
    crossing = jnp.where((i // 2) % 2 == 0, (pairing // 2) % 2, 0) - jnp.where(i == 0, CAPS[0], 0)
    kernels = [functools.partial(whole, cap) for cap in CAPS]
    return lax.switch(jnp.sum(crossing), kernels, pairing, head, conductivity, coarse_conductivity)


def solution(mesh):
    block = P("group", "dom", None, None)
    return jax.shard_map(
        per_device,
        mesh=mesh,
        in_specs=(block, block, block, P()),
        out_specs=(block, block, block),
        check_vma=False,
    )
```

```python
import functools

import jax
import jax.numpy as jnp
from jax import lax
from jax.experimental import pallas as pl
from jax.experimental.pallas import tpu as pltpu
from jax.sharding import PartitionSpec as P

MESH = pl.DeviceIdType.MESH
F32 = jnp.float32
NP = 8
CAPS = (3, 4, 5, 6, 8)

TOP = 8
CH = 32
NH = 2


FIRST = (0, 7, 1, 2)
SECOND = (3, 4, 5, 6)


def closure(h, cond, spacing):
    t = 1.5 * jnp.minimum(h, 0.0)
    r = lax.rsqrt(1.0 + t * t)
    p = t * r
    a = 1.0 + p
    k = cond * (r * lax.rsqrt(r) * (a * a))
    s2 = spacing * spacing
    w = 1.0 / (20.0 * s2 - (24.0 * s2) * (p * (r * r)))
    return k, w


def in_layer(hb, kb, x, row, rows, spacing):
    ha = hb[x, pl.ds(row, rows + 16), :]
    ka = kb[x, pl.ds(row, rows + 16), :]
    h, k = ha[8 : 8 + rows], ka[8 : 8 + rows]
    tot = (ka[9 : 9 + rows] + k) * (ha[9 : 9 + rows] - h)
    hd, kd = ha[7 : 7 + rows], ka[7 : 7 + rows]
    tot = tot + (kd + k) * (hd - h)
    n = h.shape[1]
    lane = lax.broadcasted_iota(jnp.int32, h.shape, 1)
    hz = jnp.where(lane == n - 1, 0.0, pltpu.roll(h, n - 1, 1))
    kz = jnp.where(lane == n - 1, 0.0, pltpu.roll(k, n - 1, 1))
    hs = h - spacing
    fz = (kz + k) * (hz - hs)
    fd = jnp.where(lane == 0, k * (h + spacing), pltpu.roll(fz, 1, 1))
    return h, k, tot + (fz - fd)


def kernel(cap, pairing_in, head, cond, ccond, fine_out, coarse_out, diff_out,
           hb, kb, fx, f01, f15, frecv, vs, pick, pairing,
           sbuf, sab, sx, sy, sc, sd, tbuf, tab, tx, ty, tc, td, nbuf, nab, nx, ny, nc, nd, mbuf, mab, mx, my, mc, md, bbuf, bab, bx, by, bc, bd,
           ch, ck, cfx, cf01, cf7, cfrecv,
           hsem, ksem, csem, halo_s, halo_r, sa_s, sa_r, ta_s, ta_r, na_s, na_r, ma_s, ma_r, ba_s, ba_r, sc_s, sc_r, tc_s, tc_r, nc_s, nc_r, mc_s, mc_r, bc_s, bc_r,
           cross_s, cross_r, psem):
    wb, cw, dbuf = fine_out.at[0], coarse_out.at[0], diff_out.at[0]
    g = lax.axis_index("group")
    d = lax.axis_index("dom")
    zh = lax.rem(g // 2, 2)
    me = (g // 4) * 2 + lax.rem(g, 2)

    def index_of(j, plane):
        return (j // 2) * 4 + plane * 2 + lax.rem(j, 2)

    def mate(s):
        j = lax.rem(me + s, NP)
        return j, index_of(j, zh)

    other = index_of(me, 1 - zh)
    last = 7

    def load(src, dst, sem):
        return pltpu.make_async_copy(src, dst, sem)

    def hload(l):
        return load(head.at[0, pl.ds(2 * l, 2)], hb.at[pl.ds(2 * l, 2), pl.ds(TOP, 128), :], hsem.at[l])

    def kload(l):
        return load(cond.at[0, pl.ds(2 * l, 2)], kb.at[pl.ds(2 * l, 2), pl.ds(TOP, 128), :], ksem.at[l])

    cload = load(ccond.at[0], ck.at[pl.ds(0, 8), pl.ds(8, 64), :], csem)
    bar = pltpu.get_barrier_semaphore()

    def greet(g2, d2):
        pl.semaphore_signal(bar, inc=1, device_id=(g2, d2), device_id_type=MESH)

    for s in range(1, NP):
        greet(mate(s)[1], d)
    greet(other, d)

    @pl.when(d > 0)
    def _():
        greet(g, d - 1)

    @pl.when(d < last)
    def _():
        greet(g, d + 1)

    pload = load(pairing_in, pairing, psem)
    hload(0).start()
    kload(0).start()
    pload.start()
    for l in range(1, 8):
        hload(l).start()
    for l in range(1, 8):
        kload(l).start()
    cload.start()

    def remote(src, dst, ssem, rsem, g2, d2):
        return pltpu.make_async_remote_copy(src_ref=src, dst_ref=dst, send_sem=ssem, recv_sem=rsem,
                                            device_id=(g2, d2), device_id_type=MESH)

    down = d - 1
    upper = d + 1

    def part(i, first):
        return pl.ds(first + i * (128 // NH), 128 // NH)

    halo_h = [remote(hb.at[0, part(i, TOP), :], hb.at[16, part(i, TOP), :], halo_s.at[i], halo_r.at[i], g, down) for i in range(NH)]
    halo_k = [remote(kb.at[0, part(i, TOP), :], kb.at[16, part(i, TOP), :], halo_s.at[NH + i], halo_r.at[NH + i], g, down)
              for i in range(NH)]
    halo_f = [remote(f15.at[part(i, 0), :], frecv.at[part(i, 0), :], halo_s.at[2 * NH + i], halo_r.at[2 * NH + i], g, upper)
              for i in range(NH)]
    crow = pl.ds(8, 64)
    chalo_h = remote(ch.at[0, crow, :], ch.at[8, crow, :], halo_s.at[3 * NH], halo_r.at[3 * NH], g, down)
    chalo_k = remote(ck.at[0, crow, :], ck.at[8, crow, :], halo_s.at[3 * NH + 1], halo_r.at[3 * NH + 1], g, down)
    chalo_f = remote(cf7, cfrecv, halo_s.at[3 * NH + 2], halo_r.at[3 * NH + 2], g, upper)

    def on(condition, act):
        pl.when(condition)(act)

    def chunks(act, first=0, rows=128):
        def body(i, _):
            act(pl.multiple_of(first + i * CH, CH))
            return 0

        lax.fori_loop(0, rows // CH, body, 0)

    def halo_start():
        def act():
            for i in range(NH):
                halo_h[i].start()
                halo_k[i].start()

        on(d > 0, act)

    def restrict(a, b, store):
        for r in range(0, 128, CH):
            s = a(r) + b(r)
            for q in range(4):
                vs[q, r : r + CH, :] = s[:, q * 128 : (q + 1) * 128]
        for half in range(2):
            parts = [vs[q, pl.ds(0, 64, 2), :] + vs[q, pl.ds(1, 64, 2), :] for q in (2 * half, 2 * half + 1)]
            e = jnp.concatenate(parts, axis=1)
            hi = e.astype(jnp.bfloat16)
            lo = (e - hi.astype(F32)).astype(jnp.bfloat16)
            w = pick[...]
            o = jnp.dot(hi, w, preferred_element_type=F32) + jnp.dot(lo, w, preferred_element_type=F32)
            store(half, o)

    def into(buf, pos):
        def store(half, o):
            buf[:, pos, :, half * 128 : (half + 1) * 128] = o.reshape(8, 8, 128)

        return store

    def scatter(buf, to, ssem, rsem):
        for s in range(1, NP):
            j, g2 = mate(s)
            remote(buf.at[j], to.at[me], ssem, rsem, g2, d).start()
        to[me] = buf[me]

    def scattered(buf, to, ssem, rsem):
        most = pl.ds(0, NP - 1)
        remote(buf.at[most], to.at[most], ssem, rsem, mate(1)[1], d).wait()

    def a_start(p):
        scatter(p.buf, p.ab, p.a_s, p.a_r)

    def b_copy(p):
        return remote(p.x, p.y, cross_s.at[p.i], cross_r.at[p.i], other, d)

    def b_start(p):
        scattered(p.buf, p.ab, p.a_s, p.a_r)
        for n in range(cap):
            p.x[n] = p.ab[cross[n]]
        b_copy(p).start()

    def c_start(p):
        b_copy(p).wait()
        for j in range(NP):
            mine, slot, crossed = where[j]
            p.c[j] = jnp.where(mine, p.ab[slot], p.y[crossed])
        scatter(p.c, p.to, p.c_s, p.c_r)

    def c_wait(p):
        scattered(p.c, p.to, p.c_s, p.c_r)

    start = Payload(0, sbuf, sab, sx, sy, sc, sd, sa_s, sa_r, sc_s, sc_r)
    second = Payload(3, tbuf, tab, tx, ty, tc, td, ta_s, ta_r, tc_s, tc_r)
    inner = Payload(1, nbuf, nab, nx, ny, nc, nd, na_s, na_r, nc_s, nc_r)
    more = Payload(4, mbuf, mab, mx, my, mc, md, ma_s, ma_r, mc_s, mc_r)
    outer = Payload(2, bbuf, bab, bx, by, bc, bd, ba_s, ba_r, bc_s, bc_r)

    def spot(l):
        return (start, FIRST.index(l)) if l in FIRST else (second, SECOND.index(l))

    def start_small(l):
        if l:
            hload(l).wait()
        p, pos = spot(l)
        restrict(lambda r: hb[2 * l, pl.ds(TOP + r, CH), :], lambda r: hb[2 * l + 1, pl.ds(TOP + r, CH), :], into(p.buf, pos))

    def close(x):
        def act(r):
            k, w = closure(hb[x, pl.ds(TOP + r, CH), :], kb[x, pl.ds(TOP + r, CH), :], 1.0)
            kb[x, pl.ds(TOP + r, CH), :] = k
            wb[x, pl.ds(r, CH), :] = w

        chunks(act)

    def face(x, r):
        here, there = (x, pl.ds(TOP + r, CH), slice(None)), (x + 1, pl.ds(TOP + r, CH), slice(None))
        return (kb[there] + kb[here]) * (hb[there] - hb[here])

    def first_face():
        def act(r):
            f = face(0, r)
            f01[pl.ds(r, CH), :] = f
            fx[pl.ds(r, CH), :] = f

        chunks(act)

    def step(x):
        def act(r):
            h, k, tot = in_layer(hb, kb, x, r, CH, 1.0)
            f = (kb[x + 1, pl.ds(TOP + r, CH), :] + k) * (hb[x + 1, pl.ds(TOP + r, CH), :] - h)
            tot = tot + (f - fx[pl.ds(r, CH), :])
            fx[pl.ds(r, CH), :] = f
            wb[x, pl.ds(r, CH), :] = h + tot * wb[x, pl.ds(r, CH), :]

        chunks(act)

    def step_between(x, above, below):
        def act(r):
            h, k, tot = in_layer(hb, kb, x, r, CH, 1.0)
            tot = tot + (above[pl.ds(r, CH), :] - below[pl.ds(r, CH), :])
            wb[x, pl.ds(r, CH), :] = h + tot * wb[x, pl.ds(r, CH), :]

        chunks(act)

    def upper_face(i):
        def arrived():
            halo_h[i].wait_recv()
            halo_k[i].wait_recv()

        on(d < last, arrived)

        def act(r):
            f15[pl.ds(r, CH), :] = face(15, r)

        chunks(act, i * (128 // NH), 128 // NH)
        on(d < last, halo_f[i].start)

    def lower_face():
        def arrived():
            for c in halo_f:
                c.wait_recv()

        on(d > 0, arrived)

        def edge():
            def act(r):
                frecv[pl.ds(r, CH), :] = hb[0, pl.ds(TOP + r, CH), :] * kb[0, pl.ds(TOP + r, CH), :]

            chunks(act)

        on(d == 0, edge)

    def next_small(l, buf, pos):
        restrict(lambda r: wb[2 * l, pl.ds(r, CH), :], lambda r: wb[2 * l + 1, pl.ds(r, CH), :], into(buf, pos))

    def close_coarse(l):
        p, pos = spot(l)
        h = p.to[:, pos].reshape(64, 256)
        k, w = closure(h, ck[l, crow, :], 2.0)
        ch[l, crow, :] = h
        ck[l, crow, :] = k
        cw[l] = w

    def chalo_start():
        def act():
            chalo_h.start()
            chalo_k.start()

        on(d > 0, act)

    def cface(x):
        return (ck[x + 1, crow, :] + ck[x, crow, :]) * (ch[x + 1, crow, :] - ch[x, crow, :])

    def first_cface():
        f = cface(0)
        cf01[...] = f
        cfx[...] = f

    def step_coarse(x):
        h, k, tot = in_layer(ch, ck, x, 0, 64, 2.0)
        f = cface(x)
        tot = tot + (f - cfx[...])
        cfx[...] = f
        cw[x] = h + tot * cw[x]

    def step_coarse_between(x, above, below):
        h, k, tot = in_layer(ch, ck, x, 0, 64, 2.0)
        cw[x] = h + (tot + (above[...] - below[...])) * cw[x]

    def upper_cface():
        def arrived():
            chalo_h.wait_recv()
            chalo_k.wait_recv()

        on(d < last, arrived)
        cf7[...] = cface(7)
        on(d < last, chalo_f.start)

    def lower_cface():
        on(d > 0, chalo_f.wait_recv)

        def edge():
            cfrecv[...] = ch[0, crow, :] * ck[0, crow, :]

        on(d == 0, edge)

    def difference(l, to, pos):
        dbuf[l] = to[:, pos].reshape(64, 256) - cw[l]

    def pair(l):
        if l < 6:
            kload(l + 1).wait()
        close(2 * l + 1)
        close(2 * l + 2)
        step(2 * l)
        step(2 * l + 1)
        next_small(l, nbuf if l < 5 else mbuf, (l - 1) % 4)

    def down_sent():
        for c in halo_h + halo_k:
            c.wait_send()
        chalo_h.wait_send()
        chalo_k.wait_send()

    def up_sent():
        for c in halo_f:
            c.wait_send()
        chalo_f.wait_send()

    hload(0).wait()
    kload(0).wait()
    close(0)
    pload.wait()
    cross = [jnp.int32(0)] * cap
    count = jnp.int32(0)
    for j in range(NP):
        p = pairing[index_of(j, 1 - zh)]
        mine = lax.rem(p // 2, 2) == zh
        slot = (p // 4) * 2 + lax.rem(p, 2)
        for i in range(cap):
            cross[i] = jnp.where(mine & (count == i), slot, cross[i])
        count = count + jnp.where(mine, 1, 0)
    where = []
    count = jnp.int32(0)
    for j in range(NP):
        p = pairing[index_of(j, zh)]
        mine = lax.rem(p // 2, 2) == zh
        where.append((mine, (p // 4) * 2 + lax.rem(p, 2), jnp.minimum(count, cap - 1)))
        count = count + jnp.where(mine, 0, 1)

    pi = lax.broadcasted_iota(jnp.int32, (256, 128), 0)
    pj = lax.broadcasted_iota(jnp.int32, (256, 128), 1)
    pick[...] = jnp.where(pi // 2 == pj, 0.125, 0.0).astype(jnp.bfloat16)

    for l in FIRST[:1]:
        start_small(l)
    pl.semaphore_wait(bar, NP + jnp.where(d > 0, 1, 0) + jnp.where(d < last, 1, 0))
    halo_start()
    z8 = jnp.zeros((8, 512), F32)
    zc = jnp.zeros((8, 256), F32)

    def pads(x, _):
        for b in (hb, kb):
            b[x, 0:8, :] = z8
            b[x, 136:144, :] = z8
        return 0

    lax.fori_loop(0, 16, pads, 0)

    def cpads(x, _):
        for b in (ch, ck):
            b[x, 0:8, :] = zc
            b[x, 72:80, :] = zc
        return 0

    lax.fori_loop(0, 8, cpads, 0)
    @pl.when(d == last)
    def _():
        def zero(i, _):
            hb[16, pl.ds(TOP + i * 8, 8), :] = z8
            kb[16, pl.ds(TOP + i * 8, 8), :] = z8
            return 0

        lax.fori_loop(0, 16, zero, 0)

        def czero(i, _):
            ch[8, pl.ds(8 + i * 8, 8), :] = zc
            ck[8, pl.ds(8 + i * 8, 8), :] = zc
            return 0

        lax.fori_loop(0, 8, czero, 0)

    for l in FIRST[1:]:
        start_small(l)
    a_start(start)
    for l in SECOND:
        start_small(l)
    a_start(second)
    close(1)
    first_face()
    kload(7).wait()
    close(15)
    kload(1).wait()
    close(2)
    step(1)
    pair(1)
    pair(2)
    pair(3)
    b_start(start)
    upper_face(0)
    pair(4)
    a_start(inner)
    b_start(second)
    pair(5)
    upper_face(1)
    pair(6)
    a_start(more)
    b_start(inner)
    step(14)
    step_between(15, f15, fx)
    next_small(7, bbuf, 1)
    c_start(start)
    lower_face()
    step_between(0, f01, frecv)
    next_small(0, bbuf, 0)
    a_start(outer)
    b_start(more)
    c_wait(start)
    cload.wait()
    for l in FIRST:
        close_coarse(l)
    b_start(outer)
    chalo_start()
    c_start(second)
    c_start(inner)
    c_start(more)
    c_start(outer)
    c_wait(second)
    for l in SECOND:
        close_coarse(l)
    first_cface()
    for x in range(1, 7):
        step_coarse(x)
    upper_cface()
    step_coarse_between(7, cf7, cfx)
    c_wait(inner)
    for l in range(1, 5):
        difference(l, nd, l - 1)
    c_wait(more)
    for l in range(5, 7):
        difference(l, md, l - 5)
    lower_cface()
    step_coarse_between(0, cf01, cfrecv)
    on(d > 0, down_sent)
    on(d < last, up_sent)
    c_wait(outer)
    difference(0, bd, 0)
    difference(7, bd, 1)


class Payload:
    def __init__(self, i, buf, ab, x, y, c, to, a_s, a_r, c_s, c_r):
        self.i, self.buf, self.ab, self.x, self.y, self.c, self.to = i, buf, ab, x, y, c, to
        self.a_s, self.a_r, self.c_s, self.c_r = a_s, a_r, c_s, c_r


def payload(cap, layers):
    piece = (layers, 8, 256)
    return [
        pltpu.VMEM((NP,) + piece, F32),
        pltpu.VMEM((NP,) + piece, F32),
        pltpu.VMEM((cap,) + piece, F32),
        pltpu.VMEM((cap,) + piece, F32),
        pltpu.VMEM((NP,) + piece, F32),
        pltpu.VMEM((NP,) + piece, F32),
    ]


def run(cap, pairing, head, cond, ccond):
    dma = pltpu.SemaphoreType.DMA
    scratch = [
        pltpu.VMEM((17, 144, 512), F32),
        pltpu.VMEM((17, 144, 512), F32),
        *[pltpu.VMEM((128, 512), F32)] * 4,
        pltpu.VMEM((4, 128, 128), F32),
        pltpu.VMEM((256, 128), jnp.bfloat16),
        pltpu.SMEM((16,), jnp.int32),
        *payload(cap, 4),
        *payload(cap, 4),
        *payload(cap, 4),
        *payload(cap, 2),
        *payload(cap, 2),
        pltpu.VMEM((9, 80, 256), F32),
        pltpu.VMEM((9, 80, 256), F32),
        *[pltpu.VMEM((64, 256), F32)] * 4,
        dma((8,)), dma((8,)), dma, dma((3 * NH + 3,)), dma((3 * NH + 3,)),
        *[dma] * 20,
        dma((5,)), dma((5,)), dma,
    ]
    return pl.pallas_call(
        functools.partial(kernel, cap),
        out_shape=(pltpu.VMEM(head.shape, F32), pltpu.VMEM(ccond.shape, F32), pltpu.VMEM(ccond.shape, F32)),
        in_specs=[pl.BlockSpec(memory_space=pltpu.HBM)] * 4,
        out_specs=(pl.BlockSpec(memory_space=pltpu.VMEM),) * 3,
        scratch_shapes=scratch,
        compiler_params=pltpu.CompilerParams(
            collective_id=cap, has_side_effects=True, vmem_limit_bytes=48 * 2**20
        ),
    )(*[pltpu.with_memory_space_constraint(v, pltpu.HBM) for v in (pairing, head, cond, ccond)])


def write_out(fine, coarse, diff, fine_out, coarse_out, diff_out, sem):
    copies = [pltpu.make_async_copy(fine.at[0, pl.ds(4 * i, 4)], fine_out.at[0, pl.ds(4 * i, 4)], sem.at[i]) for i in range(4)]
    copies.append(pltpu.make_async_copy(coarse, coarse_out, sem.at[4]))
    copies.append(pltpu.make_async_copy(diff, diff_out, sem.at[5]))
    for c in copies:
        c.start()
    for c in copies:
        c.wait()


def finish(*results):
    anywhere = pl.BlockSpec(memory_space=pl.ANY)
    return pl.pallas_call(
        write_out,
        out_shape=tuple(pltpu.HBM(r.shape, r.dtype) for r in results),
        in_specs=[anywhere] * 3,
        out_specs=(anywhere,) * 3,
        scratch_shapes=[pltpu.SemaphoreType.DMA((6,))],
        compiler_params=pltpu.CompilerParams(vmem_limit_bytes=2**20),
    )(*[pltpu.with_memory_space_constraint(r, pltpu.VMEM) for r in results])


def whole(cap, *arrays):
    return finish(*run(cap, *arrays))


def per_device(head, conductivity, coarse_conductivity, pairing):
    i = jnp.arange(16)
    crossing = jnp.where((i // 2) % 2 == 0, (pairing // 2) % 2, 0) - jnp.where(i == 0, CAPS[0], 0)
    kernels = [functools.partial(whole, cap) for cap in CAPS]
    return lax.switch(jnp.sum(crossing), kernels, pairing, head, conductivity, coarse_conductivity)


def solution(mesh):
    block = P("group", "dom", None, None)
    return jax.shard_map(
        per_device,
        mesh=mesh,
        in_specs=(block, block, block, P()),
        out_specs=(block, block, block),
        check_vma=False,
    )
```

```python
import functools

import jax
import jax.numpy as jnp
from jax import lax
from jax.experimental import pallas as pl
from jax.experimental.pallas import tpu as pltpu
from jax.sharding import PartitionSpec as P

MESH = pl.DeviceIdType.MESH
F32 = jnp.float32
NP = 8
CAPS = (3, 4, 5, 6, 8)

TOP = 8
CH = 32
NH = 2


FIRST = (0, 7, 1, 2)
SECOND = (3, 4, 5, 6)


def closure(h, cond, spacing):
    t = 1.5 * jnp.minimum(h, 0.0)
    r = lax.rsqrt(1.0 + t * t)
    p = t * r
    a = 1.0 + p
    k = cond * (r * lax.rsqrt(r) * (a * a))
    s2 = spacing * spacing
    w = 1.0 / (20.0 * s2 - (24.0 * s2) * (p * (r * r)))
    return k, w


def in_layer(hb, kb, x, row, rows, spacing):
    ha = hb[x, pl.ds(row, rows + 16), :]
    ka = kb[x, pl.ds(row, rows + 16), :]
    h, k = ha[8 : 8 + rows], ka[8 : 8 + rows]
    tot = (ka[9 : 9 + rows] + k) * (ha[9 : 9 + rows] - h)
    hd, kd = ha[7 : 7 + rows], ka[7 : 7 + rows]
    tot = tot + (kd + k) * (hd - h)
    n = h.shape[1]
    lane = lax.broadcasted_iota(jnp.int32, h.shape, 1)
    hz = jnp.where(lane == n - 1, 0.0, pltpu.roll(h, n - 1, 1))
    kz = jnp.where(lane == n - 1, 0.0, pltpu.roll(k, n - 1, 1))
    hs = h - spacing
    fz = (kz + k) * (hz - hs)
    fd = jnp.where(lane == 0, k * (h + spacing), pltpu.roll(fz, 1, 1))
    return h, k, tot + (fz - fd)


def kernel(cap, pairing_in, head, cond, ccond, fine_out, coarse_out, diff_out,
           hb, kb, fx, f01, f15, frecv, vs, pick, pairing,
           sbuf, sab, sx, sy, sc, sd, tbuf, tab, tx, ty, tc, td, nbuf, nab, nx, ny, nc, nd, mbuf, mab, mx, my, mc, md, bbuf, bab, bx, by, bc, bd,
           ch, ck, cfx, cf01, cf7, cfrecv,
           hsem, ksem, csem, halo_s, halo_r, sa_s, sa_r, ta_s, ta_r, na_s, na_r, ma_s, ma_r, ba_s, ba_r, sc_s, sc_r, tc_s, tc_r, nc_s, nc_r, mc_s, mc_r, bc_s, bc_r,
           cross_s, cross_r, psem):
    wb, cw, dbuf = fine_out.at[0], coarse_out.at[0], diff_out.at[0]
    g = lax.axis_index("group")
    d = lax.axis_index("dom")
    zh = lax.rem(g // 2, 2)
    me = (g // 4) * 2 + lax.rem(g, 2)

    def index_of(j, plane):
        return (j // 2) * 4 + plane * 2 + lax.rem(j, 2)

    def mate(s):
        j = lax.rem(me + s, NP)
        return j, index_of(j, zh)

    other = index_of(me, 1 - zh)
    last = 7

    def load(src, dst, sem):
        return pltpu.make_async_copy(src, dst, sem)

    def hload(l):
        return load(head.at[0, pl.ds(2 * l, 2)], hb.at[pl.ds(2 * l, 2), pl.ds(TOP, 128), :], hsem.at[l])

    def kload(l):
        return load(cond.at[0, pl.ds(2 * l, 2)], kb.at[pl.ds(2 * l, 2), pl.ds(TOP, 128), :], ksem.at[l])

    cload = load(ccond.at[0], ck.at[pl.ds(0, 8), pl.ds(8, 64), :], csem)
    bar = pltpu.get_barrier_semaphore()

    def greet(g2, d2):
        pl.semaphore_signal(bar, inc=1, device_id=(g2, d2), device_id_type=MESH)

    for s in range(1, NP):
        greet(mate(s)[1], d)
    greet(other, d)

    @pl.when(d > 0)
    def _():
        greet(g, d - 1)

    @pl.when(d < last)
    def _():
        greet(g, d + 1)

    pload = load(pairing_in, pairing, psem)
    hload(0).start()
    kload(0).start()
    pload.start()
    for l in range(1, 8):
        hload(l).start()
    for l in range(1, 8):
        kload(l).start()
    cload.start()

    def remote(src, dst, ssem, rsem, g2, d2):
        return pltpu.make_async_remote_copy(src_ref=src, dst_ref=dst, send_sem=ssem, recv_sem=rsem,
                                            device_id=(g2, d2), device_id_type=MESH)

    down = d - 1
    upper = d + 1

    def part(i, first):
        return pl.ds(first + i * (128 // NH), 128 // NH)

    halo_h = [remote(hb.at[0, part(i, TOP), :], hb.at[16, part(i, TOP), :], halo_s.at[i], halo_r.at[i], g, down) for i in range(NH)]
    halo_k = [remote(kb.at[0, part(i, TOP), :], kb.at[16, part(i, TOP), :], halo_s.at[NH + i], halo_r.at[NH + i], g, down)
              for i in range(NH)]
    halo_f = [remote(f15.at[part(i, 0), :], frecv.at[part(i, 0), :], halo_s.at[2 * NH + i], halo_r.at[2 * NH + i], g, upper)
              for i in range(NH)]
    crow = pl.ds(8, 64)
    chalo_h = remote(ch.at[0, crow, :], ch.at[8, crow, :], halo_s.at[3 * NH], halo_r.at[3 * NH], g, down)
    chalo_k = remote(ck.at[0, crow, :], ck.at[8, crow, :], halo_s.at[3 * NH + 1], halo_r.at[3 * NH + 1], g, down)
    chalo_f = remote(cf7, cfrecv, halo_s.at[3 * NH + 2], halo_r.at[3 * NH + 2], g, upper)

    def on(condition, act):
        pl.when(condition)(act)

    def chunks(act, first=0, rows=128):
        def body(i, _):
            act(pl.multiple_of(first + i * CH, CH))
            return 0

        lax.fori_loop(0, rows // CH, body, 0)

    def halo_start():
        def act():
            for i in range(NH):
                halo_h[i].start()
                halo_k[i].start()

        on(d > 0, act)

    def restrict(a, b, store):
        for r in range(0, 128, CH):
            s = a(r) + b(r)
            for q in range(4):
                vs[q, r : r + CH, :] = s[:, q * 128 : (q + 1) * 128]
        for half in range(2):
            parts = [vs[q, pl.ds(0, 64, 2), :] + vs[q, pl.ds(1, 64, 2), :] for q in (2 * half, 2 * half + 1)]
            e = jnp.concatenate(parts, axis=1)
            hi = e.astype(jnp.bfloat16)
            lo = (e - hi.astype(F32)).astype(jnp.bfloat16)
            w = pick[...]
            o = jnp.dot(hi, w, preferred_element_type=F32) + jnp.dot(lo, w, preferred_element_type=F32)
            store(half, o)

    def into(buf, pos):
        def store(half, o):
            buf[:, pos, :, half * 128 : (half + 1) * 128] = o.reshape(8, 8, 128)

        return store

    def scatter(buf, to, ssem, rsem):
        for s in range(1, NP):
            j, g2 = mate(s)
            remote(buf.at[j], to.at[me], ssem, rsem, g2, d).start()
        to[me] = buf[me]

    def scattered(buf, to, ssem, rsem):
        most = pl.ds(0, NP - 1)
        remote(buf.at[most], to.at[most], ssem, rsem, mate(1)[1], d).wait()

    def a_start(p):
        scatter(p.buf, p.ab, p.a_s, p.a_r)

    def b_copy(p):
        return remote(p.x, p.y, cross_s.at[p.i], cross_r.at[p.i], other, d)

    def b_start(p):
        scattered(p.buf, p.ab, p.a_s, p.a_r)
        for n in range(cap):
            p.x[n] = p.ab[cross[n]]
        b_copy(p).start()

    def c_start(p):
        b_copy(p).wait()
        for j in range(NP):
            mine, slot, crossed = where[j]
            p.c[j] = jnp.where(mine, p.ab[slot], p.y[crossed])
        scatter(p.c, p.to, p.c_s, p.c_r)

    def c_wait(p):
        scattered(p.c, p.to, p.c_s, p.c_r)

    start = Payload(0, sbuf, sab, sx, sy, sc, sd, sa_s, sa_r, sc_s, sc_r)
    second = Payload(3, tbuf, tab, tx, ty, tc, td, ta_s, ta_r, tc_s, tc_r)
    inner = Payload(1, nbuf, nab, nx, ny, nc, nd, na_s, na_r, nc_s, nc_r)
    more = Payload(4, mbuf, mab, mx, my, mc, md, ma_s, ma_r, mc_s, mc_r)
    outer = Payload(2, bbuf, bab, bx, by, bc, bd, ba_s, ba_r, bc_s, bc_r)

    def spot(l):
        return (start, FIRST.index(l)) if l in FIRST else (second, SECOND.index(l))

    def start_small(l):
        if l:
            hload(l).wait()
        p, pos = spot(l)
        restrict(lambda r: hb[2 * l, pl.ds(TOP + r, CH), :], lambda r: hb[2 * l + 1, pl.ds(TOP + r, CH), :], into(p.buf, pos))

    def close(x):
        def act(r):
            k, w = closure(hb[x, pl.ds(TOP + r, CH), :], kb[x, pl.ds(TOP + r, CH), :], 1.0)
            kb[x, pl.ds(TOP + r, CH), :] = k
            wb[x, pl.ds(r, CH), :] = w

        chunks(act)

    def face(x, r):
        here, there = (x, pl.ds(TOP + r, CH), slice(None)), (x + 1, pl.ds(TOP + r, CH), slice(None))
        return (kb[there] + kb[here]) * (hb[there] - hb[here])

    def first_face():
        def act(r):
            f = face(0, r)
            f01[pl.ds(r, CH), :] = f
            fx[pl.ds(r, CH), :] = f

        chunks(act)

    def step(x):
        def act(r):
            h, k, tot = in_layer(hb, kb, x, r, CH, 1.0)
            f = (kb[x + 1, pl.ds(TOP + r, CH), :] + k) * (hb[x + 1, pl.ds(TOP + r, CH), :] - h)
            tot = tot + (f - fx[pl.ds(r, CH), :])
            fx[pl.ds(r, CH), :] = f
            wb[x, pl.ds(r, CH), :] = h + tot * wb[x, pl.ds(r, CH), :]

        chunks(act)

    def step_between(x, above, below):
        def act(r):
            h, k, tot = in_layer(hb, kb, x, r, CH, 1.0)
            tot = tot + (above[pl.ds(r, CH), :] - below[pl.ds(r, CH), :])
            wb[x, pl.ds(r, CH), :] = h + tot * wb[x, pl.ds(r, CH), :]

        chunks(act)

    def upper_face(i):
        def arrived():
            halo_h[i].wait_recv()
            halo_k[i].wait_recv()

        on(d < last, arrived)

        def act(r):
            f15[pl.ds(r, CH), :] = face(15, r)

        chunks(act, i * (128 // NH), 128 // NH)
        on(d < last, halo_f[i].start)

    def lower_face():
        def arrived():
            for c in halo_f:
                c.wait_recv()

        on(d > 0, arrived)

        def edge():
            def act(r):
                frecv[pl.ds(r, CH), :] = hb[0, pl.ds(TOP + r, CH), :] * kb[0, pl.ds(TOP + r, CH), :]

            chunks(act)

        on(d == 0, edge)

    def next_small(l, buf, pos):
        restrict(lambda r: wb[2 * l, pl.ds(r, CH), :], lambda r: wb[2 * l + 1, pl.ds(r, CH), :], into(buf, pos))

    def close_coarse(l):
        p, pos = spot(l)
        h = p.to[:, pos].reshape(64, 256)
        k, w = closure(h, ck[l, crow, :], 2.0)
        ch[l, crow, :] = h
        ck[l, crow, :] = k
        cw[l] = w

    def chalo_start():
        def act():
            chalo_h.start()
            chalo_k.start()

        on(d > 0, act)

    def cface(x):
        return (ck[x + 1, crow, :] + ck[x, crow, :]) * (ch[x + 1, crow, :] - ch[x, crow, :])

    def first_cface():
        f = cface(0)
        cf01[...] = f
        cfx[...] = f

    def step_coarse(x):
        h, k, tot = in_layer(ch, ck, x, 0, 64, 2.0)
        f = cface(x)
        tot = tot + (f - cfx[...])
        cfx[...] = f
        cw[x] = h + tot * cw[x]

    def step_coarse_between(x, above, below):
        h, k, tot = in_layer(ch, ck, x, 0, 64, 2.0)
        cw[x] = h + (tot + (above[...] - below[...])) * cw[x]

    def upper_cface():
        def arrived():
            chalo_h.wait_recv()
            chalo_k.wait_recv()

        on(d < last, arrived)
        cf7[...] = cface(7)
        on(d < last, chalo_f.start)

    def lower_cface():
        on(d > 0, chalo_f.wait_recv)

        def edge():
            cfrecv[...] = ch[0, crow, :] * ck[0, crow, :]

        on(d == 0, edge)

    def difference(l, to, pos):
        dbuf[l] = to[:, pos].reshape(64, 256) - cw[l]

    def pair(l):
        if l < 6:
            kload(l + 1).wait()
        close(2 * l + 1)
        close(2 * l + 2)
        step(2 * l)
        step(2 * l + 1)
        next_small(l, nbuf if l < 5 else mbuf, (l - 1) % 4)

    def down_sent():
        for c in halo_h + halo_k:
            c.wait_send()
        chalo_h.wait_send()
        chalo_k.wait_send()

    def up_sent():
        for c in halo_f:
            c.wait_send()
        chalo_f.wait_send()

    hload(0).wait()
    kload(0).wait()
    close(0)
    pload.wait()
    cross = [jnp.int32(0)] * cap
    count = jnp.int32(0)
    for j in range(NP):
        p = pairing[index_of(j, 1 - zh)]
        mine = lax.rem(p // 2, 2) == zh
        slot = (p // 4) * 2 + lax.rem(p, 2)
        for i in range(cap):
            cross[i] = jnp.where(mine & (count == i), slot, cross[i])
        count = count + jnp.where(mine, 1, 0)
    where = []
    count = jnp.int32(0)
    for j in range(NP):
        p = pairing[index_of(j, zh)]
        mine = lax.rem(p // 2, 2) == zh
        where.append((mine, (p // 4) * 2 + lax.rem(p, 2), jnp.minimum(count, cap - 1)))
        count = count + jnp.where(mine, 0, 1)

    pi = lax.broadcasted_iota(jnp.int32, (256, 128), 0)
    pj = lax.broadcasted_iota(jnp.int32, (256, 128), 1)
    pick[...] = jnp.where(pi // 2 == pj, 0.125, 0.0).astype(jnp.bfloat16)

    for l in FIRST[:1]:
        start_small(l)
    pl.semaphore_wait(bar, NP + jnp.where(d > 0, 1, 0) + jnp.where(d < last, 1, 0))
    halo_start()
    z8 = jnp.zeros((8, 512), F32)
    zc = jnp.zeros((8, 256), F32)

    def pads(x, _):
        for b in (hb, kb):
            b[x, 0:8, :] = z8
            b[x, 136:144, :] = z8
        return 0

    lax.fori_loop(0, 16, pads, 0)

    def cpads(x, _):
        for b in (ch, ck):
            b[x, 0:8, :] = zc
            b[x, 72:80, :] = zc
        return 0

    lax.fori_loop(0, 8, cpads, 0)
    @pl.when(d == last)
    def _():
        def zero(i, _):
            hb[16, pl.ds(TOP + i * 8, 8), :] = z8
            kb[16, pl.ds(TOP + i * 8, 8), :] = z8
            return 0

        lax.fori_loop(0, 16, zero, 0)

        def czero(i, _):
            ch[8, pl.ds(8 + i * 8, 8), :] = zc
            ck[8, pl.ds(8 + i * 8, 8), :] = zc
            return 0

        lax.fori_loop(0, 8, czero, 0)

    for l in FIRST[1:]:
        start_small(l)
    a_start(start)
    for l in SECOND:
        start_small(l)
    a_start(second)
    close(1)
    first_face()
    kload(7).wait()
    close(15)
    kload(1).wait()
    close(2)
    step(1)
    pair(1)
    pair(2)
    pair(3)
    b_start(start)
    upper_face(0)
    pair(4)
    a_start(inner)
    pair(5)
    pair(6)
    a_start(more)
    upper_face(1)
    b_start(second)
    b_start(inner)
    step(14)
    step_between(15, f15, fx)
    next_small(7, bbuf, 1)
    c_start(start)
    lower_face()
    step_between(0, f01, frecv)
    next_small(0, bbuf, 0)
    a_start(outer)
    b_start(more)
    c_wait(start)
    cload.wait()
    for l in FIRST:
        close_coarse(l)
    c_start(second)
    b_start(outer)
    chalo_start()
    c_start(inner)
    c_wait(second)
    for l in SECOND:
        close_coarse(l)
    first_cface()
    for x in range(1, 7):
        step_coarse(x)
    c_start(more)
    c_start(outer)
    upper_cface()
    step_coarse_between(7, cf7, cfx)
    c_wait(inner)
    for l in range(1, 5):
        difference(l, nd, l - 1)
    c_wait(more)
    for l in range(5, 7):
        difference(l, md, l - 5)
    lower_cface()
    step_coarse_between(0, cf01, cfrecv)
    on(d > 0, down_sent)
    on(d < last, up_sent)
    c_wait(outer)
    difference(0, bd, 0)
    difference(7, bd, 1)


class Payload:
    def __init__(self, i, buf, ab, x, y, c, to, a_s, a_r, c_s, c_r):
        self.i, self.buf, self.ab, self.x, self.y, self.c, self.to = i, buf, ab, x, y, c, to
        self.a_s, self.a_r, self.c_s, self.c_r = a_s, a_r, c_s, c_r


def payload(cap, layers):
    piece = (layers, 8, 256)
    return [
        pltpu.VMEM((NP,) + piece, F32),
        pltpu.VMEM((NP,) + piece, F32),
        pltpu.VMEM((cap,) + piece, F32),
        pltpu.VMEM((cap,) + piece, F32),
        pltpu.VMEM((NP,) + piece, F32),
        pltpu.VMEM((NP,) + piece, F32),
    ]


def run(cap, pairing, head, cond, ccond):
    dma = pltpu.SemaphoreType.DMA
    scratch = [
        pltpu.VMEM((17, 144, 512), F32),
        pltpu.VMEM((17, 144, 512), F32),
        *[pltpu.VMEM((128, 512), F32)] * 4,
        pltpu.VMEM((4, 128, 128), F32),
        pltpu.VMEM((256, 128), jnp.bfloat16),
        pltpu.SMEM((16,), jnp.int32),
        *payload(cap, 4),
        *payload(cap, 4),
        *payload(cap, 4),
        *payload(cap, 2),
        *payload(cap, 2),
        pltpu.VMEM((9, 80, 256), F32),
        pltpu.VMEM((9, 80, 256), F32),
        *[pltpu.VMEM((64, 256), F32)] * 4,
        dma((8,)), dma((8,)), dma, dma((3 * NH + 3,)), dma((3 * NH + 3,)),
        *[dma] * 20,
        dma((5,)), dma((5,)), dma,
    ]
    return pl.pallas_call(
        functools.partial(kernel, cap),
        out_shape=(pltpu.VMEM(head.shape, F32), pltpu.VMEM(ccond.shape, F32), pltpu.VMEM(ccond.shape, F32)),
        in_specs=[pl.BlockSpec(memory_space=pltpu.HBM)] * 4,
        out_specs=(pl.BlockSpec(memory_space=pltpu.VMEM),) * 3,
        scratch_shapes=scratch,
        compiler_params=pltpu.CompilerParams(
            collective_id=cap, has_side_effects=True, vmem_limit_bytes=48 * 2**20
        ),
    )(*[pltpu.with_memory_space_constraint(v, pltpu.HBM) for v in (pairing, head, cond, ccond)])


def write_out(fine, coarse, diff, fine_out, coarse_out, diff_out, sem):
    copies = [pltpu.make_async_copy(fine.at[0, pl.ds(4 * i, 4)], fine_out.at[0, pl.ds(4 * i, 4)], sem.at[i]) for i in range(4)]
    copies.append(pltpu.make_async_copy(coarse, coarse_out, sem.at[4]))
    copies.append(pltpu.make_async_copy(diff, diff_out, sem.at[5]))
    for c in copies:
        c.start()
    for c in copies:
        c.wait()


def finish(*results):
    anywhere = pl.BlockSpec(memory_space=pl.ANY)
    return pl.pallas_call(
        write_out,
        out_shape=tuple(pltpu.HBM(r.shape, r.dtype) for r in results),
        in_specs=[anywhere] * 3,
        out_specs=(anywhere,) * 3,
        scratch_shapes=[pltpu.SemaphoreType.DMA((6,))],
        compiler_params=pltpu.CompilerParams(vmem_limit_bytes=2**20),
    )(*[pltpu.with_memory_space_constraint(r, pltpu.VMEM) for r in results])


def whole(cap, *arrays):
    return finish(*run(cap, *arrays))


def per_device(head, conductivity, coarse_conductivity, pairing):
    i = jnp.arange(16)
    crossing = jnp.where((i // 2) % 2 == 0, (pairing // 2) % 2, 0) - jnp.where(i == 0, CAPS[0], 0)
    kernels = [functools.partial(whole, cap) for cap in CAPS]
    return lax.switch(jnp.sum(crossing), kernels, pairing, head, conductivity, coarse_conductivity)


def solution(mesh):
    block = P("group", "dom", None, None)
    return jax.shard_map(
        per_device,
        mesh=mesh,
        in_specs=(block, block, block, P()),
        out_specs=(block, block, block),
        check_vma=False,
    )
```

```python
import functools

import jax
import jax.numpy as jnp
from jax import lax
from jax.experimental import pallas as pl
from jax.experimental.pallas import tpu as pltpu
from jax.sharding import PartitionSpec as P

MESH = pl.DeviceIdType.MESH
F32 = jnp.float32
NP = 8
CAPS = (3, 4, 5, 6, 8)

TOP = 8
CH = 32
NH = 2


FIRST = (0, 7, 1, 2)
SECOND = (3, 4, 5, 6)


def closure(h, cond, spacing):
    t = 1.5 * jnp.minimum(h, 0.0)
    r = lax.rsqrt(1.0 + t * t)
    p = t * r
    a = 1.0 + p
    k = cond * (r * lax.rsqrt(r) * (a * a))
    s2 = spacing * spacing
    w = 1.0 / (20.0 * s2 - (24.0 * s2) * (p * (r * r)))
    return k, w


def in_layer(hb, kb, x, row, rows, spacing):
    ha = hb[x, pl.ds(row, rows + 16), :]
    ka = kb[x, pl.ds(row, rows + 16), :]
    h, k = ha[8 : 8 + rows], ka[8 : 8 + rows]
    tot = (ka[9 : 9 + rows] + k) * (ha[9 : 9 + rows] - h)
    hd, kd = ha[7 : 7 + rows], ka[7 : 7 + rows]
    tot = tot + (kd + k) * (hd - h)
    n = h.shape[1]
    lane = lax.broadcasted_iota(jnp.int32, h.shape, 1)
    hz = jnp.where(lane == n - 1, 0.0, pltpu.roll(h, n - 1, 1))
    kz = jnp.where(lane == n - 1, 0.0, pltpu.roll(k, n - 1, 1))
    hs = h - spacing
    fz = (kz + k) * (hz - hs)
    fd = jnp.where(lane == 0, k * (h + spacing), pltpu.roll(fz, 1, 1))
    return h, k, tot + (fz - fd)


def kernel(cap, pairing_in, head, cond, ccond, fine_out, coarse_out, diff_out,
           hb, kb, fx, f01, f15, frecv, vs, pick, pairing,
           sbuf, sab, sx, sy, sc, sd, tbuf, tab, tx, ty, tc, td, nbuf, nab, nx, ny, nc, nd, mbuf, mab, mx, my, mc, md, bbuf, bab, bx, by, bc, bd,
           ch, ck, cfx, cf01, cf7, cfrecv,
           hsem, ksem, csem, halo_s, halo_r, sa_s, sa_r, ta_s, ta_r, na_s, na_r, ma_s, ma_r, ba_s, ba_r, sc_s, sc_r, tc_s, tc_r, nc_s, nc_r, mc_s, mc_r, bc_s, bc_r,
           cross_s, cross_r, psem):
    wb, cw, dbuf = fine_out.at[0], coarse_out.at[0], diff_out.at[0]
    g = lax.axis_index("group")
    d = lax.axis_index("dom")
    zh = lax.rem(g // 2, 2)
    me = (g // 4) * 2 + lax.rem(g, 2)

    def index_of(j, plane):
        return (j // 2) * 4 + plane * 2 + lax.rem(j, 2)

    def mate(s):
        j = lax.rem(me + s, NP)
        return j, index_of(j, zh)

    other = index_of(me, 1 - zh)
    last = 7

    def load(src, dst, sem):
        return pltpu.make_async_copy(src, dst, sem)

    def hload(l):
        return load(head.at[0, pl.ds(2 * l, 2)], hb.at[pl.ds(2 * l, 2), pl.ds(TOP, 128), :], hsem.at[l])

    def kload(l):
        return load(cond.at[0, pl.ds(2 * l, 2)], kb.at[pl.ds(2 * l, 2), pl.ds(TOP, 128), :], ksem.at[l])

    cload = load(ccond.at[0], ck.at[pl.ds(0, 8), pl.ds(8, 64), :], csem)
    bar = pltpu.get_barrier_semaphore()

    def greet(g2, d2):
        pl.semaphore_signal(bar, inc=1, device_id=(g2, d2), device_id_type=MESH)

    for s in range(1, NP):
        greet(mate(s)[1], d)
    greet(other, d)

    @pl.when(d > 0)
    def _():
        greet(g, d - 1)

    @pl.when(d < last)
    def _():
        greet(g, d + 1)

    pload = load(pairing_in, pairing, psem)
    hload(0).start()
    kload(0).start()
    pload.start()
    for l in range(1, 8):
        hload(l).start()
    for l in range(1, 8):
        kload(l).start()
    cload.start()

    def remote(src, dst, ssem, rsem, g2, d2):
        return pltpu.make_async_remote_copy(src_ref=src, dst_ref=dst, send_sem=ssem, recv_sem=rsem,
                                            device_id=(g2, d2), device_id_type=MESH)

    down = d - 1
    upper = d + 1

    def part(i, first):
        return pl.ds(first + i * (128 // NH), 128 // NH)

    halo_h = [remote(hb.at[0, part(i, TOP), :], hb.at[16, part(i, TOP), :], halo_s.at[i], halo_r.at[i], g, down) for i in range(NH)]
    halo_k = [remote(kb.at[0, part(i, TOP), :], kb.at[16, part(i, TOP), :], halo_s.at[NH + i], halo_r.at[NH + i], g, down)
              for i in range(NH)]
    halo_f = [remote(f15.at[part(i, 0), :], frecv.at[part(i, 0), :], halo_s.at[2 * NH + i], halo_r.at[2 * NH + i], g, upper)
              for i in range(NH)]
    crow = pl.ds(8, 64)
    chalo_h = remote(ch.at[0, crow, :], ch.at[8, crow, :], halo_s.at[3 * NH], halo_r.at[3 * NH], g, down)
    chalo_k = remote(ck.at[0, crow, :], ck.at[8, crow, :], halo_s.at[3 * NH + 1], halo_r.at[3 * NH + 1], g, down)
    chalo_f = remote(cf7, cfrecv, halo_s.at[3 * NH + 2], halo_r.at[3 * NH + 2], g, upper)

    def on(condition, act):
        pl.when(condition)(act)

    def chunks(act, first=0, rows=128):
        def body(i, _):
            act(pl.multiple_of(first + i * CH, CH))
            return 0

        lax.fori_loop(0, rows // CH, body, 0)

    def halo_start():
        def act():
            for i in range(NH):
                halo_h[i].start()
                halo_k[i].start()

        on(d > 0, act)

    def restrict(a, b, store):
        for r in range(0, 128, CH):
            s = a(r) + b(r)
            for q in range(4):
                vs[q, r : r + CH, :] = s[:, q * 128 : (q + 1) * 128]
        for half in range(2):
            parts = [vs[q, pl.ds(0, 64, 2), :] + vs[q, pl.ds(1, 64, 2), :] for q in (2 * half, 2 * half + 1)]
            e = jnp.concatenate(parts, axis=1)
            hi = e.astype(jnp.bfloat16)
            lo = (e - hi.astype(F32)).astype(jnp.bfloat16)
            w = pick[...]
            o = jnp.dot(hi, w, preferred_element_type=F32) + jnp.dot(lo, w, preferred_element_type=F32)
            store(half, o)

    def into(buf, pos):
        def store(half, o):
            buf[:, pos, :, half * 128 : (half + 1) * 128] = o.reshape(8, 8, 128)

        return store

    def scatter(buf, to, ssem, rsem):
        for s in range(1, NP):
            j, g2 = mate(s)
            remote(buf.at[j], to.at[me], ssem, rsem, g2, d).start()
        to[me] = buf[me]

    def scattered(buf, to, ssem, rsem):
        most = pl.ds(0, NP - 1)
        remote(buf.at[most], to.at[most], ssem, rsem, mate(1)[1], d).wait()

    def a_start(p):
        scatter(p.buf, p.ab, p.a_s, p.a_r)

    def b_copy(p):
        return remote(p.x, p.y, cross_s.at[p.i], cross_r.at[p.i], other, d)

    def b_start(p):
        scattered(p.buf, p.ab, p.a_s, p.a_r)
        for n in range(cap):
            p.x[n] = p.ab[cross[n]]
        b_copy(p).start()

    def c_start(p):
        b_copy(p).wait()
        for j in range(NP):
            mine, slot, crossed = where[j]
            p.c[j] = jnp.where(mine, p.ab[slot], p.y[crossed])
        scatter(p.c, p.to, p.c_s, p.c_r)

    def c_wait(p):
        scattered(p.c, p.to, p.c_s, p.c_r)

    start = Payload(0, sbuf, sab, sx, sy, sc, sd, sa_s, sa_r, sc_s, sc_r)
    second = Payload(3, tbuf, tab, tx, ty, tc, td, ta_s, ta_r, tc_s, tc_r)
    inner = Payload(1, nbuf, nab, nx, ny, nc, nd, na_s, na_r, nc_s, nc_r)
    more = Payload(4, mbuf, mab, mx, my, mc, md, ma_s, ma_r, mc_s, mc_r)
    outer = Payload(2, bbuf, bab, bx, by, bc, bd, ba_s, ba_r, bc_s, bc_r)

    def spot(l):
        return (start, FIRST.index(l)) if l in FIRST else (second, SECOND.index(l))

    def start_small(l):
        if l:
            hload(l).wait()
        p, pos = spot(l)
        restrict(lambda r: hb[2 * l, pl.ds(TOP + r, CH), :], lambda r: hb[2 * l + 1, pl.ds(TOP + r, CH), :], into(p.buf, pos))

    def close(x):
        def act(r):
            k, w = closure(hb[x, pl.ds(TOP + r, CH), :], kb[x, pl.ds(TOP + r, CH), :], 1.0)
            kb[x, pl.ds(TOP + r, CH), :] = k
            wb[x, pl.ds(r, CH), :] = w

        chunks(act)

    def face(x, r):
        here, there = (x, pl.ds(TOP + r, CH), slice(None)), (x + 1, pl.ds(TOP + r, CH), slice(None))
        return (kb[there] + kb[here]) * (hb[there] - hb[here])

    def first_face():
        def act(r):
            f = face(0, r)
            f01[pl.ds(r, CH), :] = f
            fx[pl.ds(r, CH), :] = f

        chunks(act)

    def step(x):
        def act(r):
            h, k, tot = in_layer(hb, kb, x, r, CH, 1.0)
            f = (kb[x + 1, pl.ds(TOP + r, CH), :] + k) * (hb[x + 1, pl.ds(TOP + r, CH), :] - h)
            tot = tot + (f - fx[pl.ds(r, CH), :])
            fx[pl.ds(r, CH), :] = f
            wb[x, pl.ds(r, CH), :] = h + tot * wb[x, pl.ds(r, CH), :]

        chunks(act)

    def step_between(x, above, below):
        def act(r):
            h, k, tot = in_layer(hb, kb, x, r, CH, 1.0)
            tot = tot + (above[pl.ds(r, CH), :] - below[pl.ds(r, CH), :])
            wb[x, pl.ds(r, CH), :] = h + tot * wb[x, pl.ds(r, CH), :]

        chunks(act)

    def upper_face(i):
        def arrived():
            halo_h[i].wait_recv()
            halo_k[i].wait_recv()

        on(d < last, arrived)

        def act(r):
            f15[pl.ds(r, CH), :] = face(15, r)

        chunks(act, i * (128 // NH), 128 // NH)
        on(d < last, halo_f[i].start)

    def lower_face():
        def arrived():
            for c in halo_f:
                c.wait_recv()

        on(d > 0, arrived)

        def edge():
            def act(r):
                frecv[pl.ds(r, CH), :] = hb[0, pl.ds(TOP + r, CH), :] * kb[0, pl.ds(TOP + r, CH), :]

            chunks(act)

        on(d == 0, edge)

    def next_small(l, buf, pos):
        restrict(lambda r: wb[2 * l, pl.ds(r, CH), :], lambda r: wb[2 * l + 1, pl.ds(r, CH), :], into(buf, pos))

    def close_coarse(l):
        p, pos = spot(l)
        h = p.to[:, pos].reshape(64, 256)
        k, w = closure(h, ck[l, crow, :], 2.0)
        ch[l, crow, :] = h
        ck[l, crow, :] = k
        cw[l] = w

    def chalo_start():
        def act():
            chalo_h.start()
            chalo_k.start()

        on(d > 0, act)

    def cface(x):
        return (ck[x + 1, crow, :] + ck[x, crow, :]) * (ch[x + 1, crow, :] - ch[x, crow, :])

    def first_cface():
        f = cface(0)
        cf01[...] = f
        cfx[...] = f

    def step_coarse(x):
        h, k, tot = in_layer(ch, ck, x, 0, 64, 2.0)
        f = cface(x)
        tot = tot + (f - cfx[...])
        cfx[...] = f
        cw[x] = h + tot * cw[x]

    def step_coarse_between(x, above, below):
        h, k, tot = in_layer(ch, ck, x, 0, 64, 2.0)
        cw[x] = h + (tot + (above[...] - below[...])) * cw[x]

    def upper_cface():
        def arrived():
            chalo_h.wait_recv()
            chalo_k.wait_recv()

        on(d < last, arrived)
        cf7[...] = cface(7)
        on(d < last, chalo_f.start)

    def lower_cface():
        on(d > 0, chalo_f.wait_recv)

        def edge():
            cfrecv[...] = ch[0, crow, :] * ck[0, crow, :]

        on(d == 0, edge)

    def difference(l, to, pos):
        dbuf[l] = to[:, pos].reshape(64, 256) - cw[l]

    def pair(l):
        if l < 6:
            kload(l + 1).wait()
        close(2 * l + 1)
        close(2 * l + 2)
        step(2 * l)
        step(2 * l + 1)
        next_small(l, nbuf if l < 5 else mbuf, (l - 1) % 4)

    def down_sent():
        for c in halo_h + halo_k:
            c.wait_send()
        chalo_h.wait_send()
        chalo_k.wait_send()

    def up_sent():
        for c in halo_f:
            c.wait_send()
        chalo_f.wait_send()

    hload(0).wait()
    kload(0).wait()
    close(0)
    pload.wait()
    cross = [jnp.int32(0)] * cap
    count = jnp.int32(0)
    for j in range(NP):
        p = pairing[index_of(j, 1 - zh)]
        mine = lax.rem(p // 2, 2) == zh
        slot = (p // 4) * 2 + lax.rem(p, 2)
        for i in range(cap):
            cross[i] = jnp.where(mine & (count == i), slot, cross[i])
        count = count + jnp.where(mine, 1, 0)
    where = []
    count = jnp.int32(0)
    for j in range(NP):
        p = pairing[index_of(j, zh)]
        mine = lax.rem(p // 2, 2) == zh
        where.append((mine, (p // 4) * 2 + lax.rem(p, 2), jnp.minimum(count, cap - 1)))
        count = count + jnp.where(mine, 0, 1)

    pi = lax.broadcasted_iota(jnp.int32, (256, 128), 0)
    pj = lax.broadcasted_iota(jnp.int32, (256, 128), 1)
    pick[...] = jnp.where(pi // 2 == pj, 0.125, 0.0).astype(jnp.bfloat16)

    for l in FIRST[:1]:
        start_small(l)
    pl.semaphore_wait(bar, NP + jnp.where(d > 0, 1, 0) + jnp.where(d < last, 1, 0))
    halo_start()
    for l in FIRST[1:]:
        start_small(l)
    a_start(start)
    z8 = jnp.zeros((8, 512), F32)
    zc = jnp.zeros((8, 256), F32)

    def pads(x, _):
        for b in (hb, kb):
            b[x, 0:8, :] = z8
            b[x, 136:144, :] = z8
        return 0

    lax.fori_loop(0, 16, pads, 0)

    def cpads(x, _):
        for b in (ch, ck):
            b[x, 0:8, :] = zc
            b[x, 72:80, :] = zc
        return 0

    lax.fori_loop(0, 8, cpads, 0)
    @pl.when(d == last)
    def _():
        def zero(i, _):
            hb[16, pl.ds(TOP + i * 8, 8), :] = z8
            kb[16, pl.ds(TOP + i * 8, 8), :] = z8
            return 0

        lax.fori_loop(0, 16, zero, 0)

        def czero(i, _):
            ch[8, pl.ds(8 + i * 8, 8), :] = zc
            ck[8, pl.ds(8 + i * 8, 8), :] = zc
            return 0

        lax.fori_loop(0, 8, czero, 0)

    for l in SECOND:
        start_small(l)
    a_start(second)
    close(1)
    first_face()
    kload(7).wait()
    close(15)
    kload(1).wait()
    close(2)
    step(1)
    pair(1)
    pair(2)
    pair(3)
    b_start(start)
    upper_face(0)
    pair(4)
    a_start(inner)
    pair(5)
    pair(6)
    a_start(more)
    upper_face(1)
    b_start(second)
    b_start(inner)
    step(14)
    step_between(15, f15, fx)
    next_small(7, bbuf, 1)
    c_start(start)
    lower_face()
    step_between(0, f01, frecv)
    next_small(0, bbuf, 0)
    a_start(outer)
    b_start(more)
    c_wait(start)
    cload.wait()
    for l in FIRST:
        close_coarse(l)
    c_start(second)
    b_start(outer)
    chalo_start()
    c_start(inner)
    c_wait(second)
    for l in SECOND:
        close_coarse(l)
    first_cface()
    for x in range(1, 7):
        step_coarse(x)
    c_start(more)
    c_start(outer)
    upper_cface()
    step_coarse_between(7, cf7, cfx)
    c_wait(inner)
    for l in range(1, 5):
        difference(l, nd, l - 1)
    c_wait(more)
    for l in range(5, 7):
        difference(l, md, l - 5)
    lower_cface()
    step_coarse_between(0, cf01, cfrecv)
    on(d > 0, down_sent)
    on(d < last, up_sent)
    c_wait(outer)
    difference(0, bd, 0)
    difference(7, bd, 1)


class Payload:
    def __init__(self, i, buf, ab, x, y, c, to, a_s, a_r, c_s, c_r):
        self.i, self.buf, self.ab, self.x, self.y, self.c, self.to = i, buf, ab, x, y, c, to
        self.a_s, self.a_r, self.c_s, self.c_r = a_s, a_r, c_s, c_r


def payload(cap, layers):
    piece = (layers, 8, 256)
    return [
        pltpu.VMEM((NP,) + piece, F32),
        pltpu.VMEM((NP,) + piece, F32),
        pltpu.VMEM((cap,) + piece, F32),
        pltpu.VMEM((cap,) + piece, F32),
        pltpu.VMEM((NP,) + piece, F32),
        pltpu.VMEM((NP,) + piece, F32),
    ]


def run(cap, pairing, head, cond, ccond):
    dma = pltpu.SemaphoreType.DMA
    scratch = [
        pltpu.VMEM((17, 144, 512), F32),
        pltpu.VMEM((17, 144, 512), F32),
        *[pltpu.VMEM((128, 512), F32)] * 4,
        pltpu.VMEM((4, 128, 128), F32),
        pltpu.VMEM((256, 128), jnp.bfloat16),
        pltpu.SMEM((16,), jnp.int32),
        *payload(cap, 4),
        *payload(cap, 4),
        *payload(cap, 4),
        *payload(cap, 2),
        *payload(cap, 2),
        pltpu.VMEM((9, 80, 256), F32),
        pltpu.VMEM((9, 80, 256), F32),
        *[pltpu.VMEM((64, 256), F32)] * 4,
        dma((8,)), dma((8,)), dma, dma((3 * NH + 3,)), dma((3 * NH + 3,)),
        *[dma] * 20,
        dma((5,)), dma((5,)), dma,
    ]
    return pl.pallas_call(
        functools.partial(kernel, cap),
        out_shape=(pltpu.VMEM(head.shape, F32), pltpu.VMEM(ccond.shape, F32), pltpu.VMEM(ccond.shape, F32)),
        in_specs=[pl.BlockSpec(memory_space=pltpu.HBM)] * 4,
        out_specs=(pl.BlockSpec(memory_space=pltpu.VMEM),) * 3,
        scratch_shapes=scratch,
        compiler_params=pltpu.CompilerParams(
            collective_id=cap, has_side_effects=True, vmem_limit_bytes=48 * 2**20
        ),
    )(*[pltpu.with_memory_space_constraint(v, pltpu.HBM) for v in (pairing, head, cond, ccond)])


def write_out(fine, coarse, diff, fine_out, coarse_out, diff_out, sem):
    copies = [pltpu.make_async_copy(fine.at[0, pl.ds(4 * i, 4)], fine_out.at[0, pl.ds(4 * i, 4)], sem.at[i]) for i in range(4)]
    copies.append(pltpu.make_async_copy(coarse, coarse_out, sem.at[4]))
    copies.append(pltpu.make_async_copy(diff, diff_out, sem.at[5]))
    for c in copies:
        c.start()
    for c in copies:
        c.wait()


def finish(*results):
    anywhere = pl.BlockSpec(memory_space=pl.ANY)
    return pl.pallas_call(
        write_out,
        out_shape=tuple(pltpu.HBM(r.shape, r.dtype) for r in results),
        in_specs=[anywhere] * 3,
        out_specs=(anywhere,) * 3,
        scratch_shapes=[pltpu.SemaphoreType.DMA((6,))],
        compiler_params=pltpu.CompilerParams(vmem_limit_bytes=2**20),
    )(*[pltpu.with_memory_space_constraint(r, pltpu.VMEM) for r in results])


def whole(cap, *arrays):
    return finish(*run(cap, *arrays))


def per_device(head, conductivity, coarse_conductivity, pairing):
    i = jnp.arange(16)
    crossing = jnp.where((i // 2) % 2 == 0, (pairing // 2) % 2, 0) - jnp.where(i == 0, CAPS[0], 0)
    kernels = [functools.partial(whole, cap) for cap in CAPS]
    return lax.switch(jnp.sum(crossing), kernels, pairing, head, conductivity, coarse_conductivity)


def solution(mesh):
    block = P("group", "dom", None, None)
    return jax.shard_map(
        per_device,
        mesh=mesh,
        in_specs=(block, block, block, P()),
        out_specs=(block, block, block),
        check_vma=False,
    )
```
